512 devices in a mesh: block: 64 (over z, y_lo, core), day: 8 (over x, y_hi).
Axes of the slice: x: 4, y: 4 (y_hi: 2, y_lo: 2; y = y_hi * 2 + y_lo), z: 16, core: 2. Of those that a mesh axis runs over, the one named last changes fastest.
Arguments:
- traces: float32 [8, 4096, 2400], P('day', 'block'), may hold values from -6 to 6
- counts: int32 [64], replicated, may hold values from 1 to 64, 3072 in all
- order: int32 [64], replicated, may hold values from 0 to 63, each once
Outputs:
- stacks: float32 [3, 64, 61, 4096], P(None, 'day', None, 'block')
The draws below stay inside these ranges and needn't reach their ends.
Inputs may be any that keep to these rules, and one draw needn't show every extreme that they name: Slots from counts[b] to 63 of block b hold no channel; some block holds exactly 64. `order`: a permutation of the blocks; the window takes its first 3 entries as owners.
All inputs are finite; a program needn't handle non-finite values.
Results may differ from the reference program's by a relative error of at most 0.0037.
Values may be sent and summed in bfloat16 or wider, within the bound.
A program may use at most 128 MiB of HBM per device.

```python
import math
import jax
import jax.numpy as jnp
import numpy as np
from jax import lax

CAP = 64
SEG = 2400
LAGS = 61
STEPS = 3
HALF = 30
TIME_BLOCK = 800
SAMP = 2400
CHANNELS = 4096
DAYS = 8
N_BLOCK = 64


def block_scale(own_key, shape, shards, least, top_value):
    def one(axis_at, blocks):
        heights = jax.random.uniform(jax.random.fold_in(jax.random.fold_in(own_key, 6), axis_at), (blocks,), jnp.float32, least / len(shards), top_value / len(shards))
        return jnp.repeat(jnp.exp(heights), shape[axis_at] // blocks).reshape((-1,) + (1,) * (len(shape) - axis_at - 1))

    factor_of = one(*shards[0])
    for cut in shards[1:]:
        factor_of = factor_of * one(*cut)
    return factor_of


def split_up(count, total, limit, skew):
    portions = [(1 << 20) // math.isqrt(standing ** skew) + 1 for standing in range(2, count + 1)]
    rest, given = total - limit - (count - 1), [1] * (count - 1)
    while rest > 0:
        movable = [i for i in range(count - 1) if given[i] < limit]
        pool, budget = sum([portions[i] for i in movable]), rest
        for i in movable:
            more = min(limit - given[i], max(1, budget * portions[i] // pool), rest)
            given[i] = given[i] + more
            rest = rest - more
    return np.array([limit] + given)


def ragged(key, count, total, limit, slope):
    if count == 2:
        one = jax.random.randint(key, (), max(1, total - limit), min(limit, total - 1) + 1)
        return jnp.stack([one, total - one])
    tallies = jnp.asarray(split_up(count, total, limit, slope), jnp.int32)
    couples = (count - 1) // 2
    source_of, taker = tallies[1:1 + 2 * couples:2], tallies[2:2 + 2 * couples:2]
    slack = jnp.minimum(source_of - 1, limit - taker)
    passed = jax.random.randint(jax.random.fold_in(key, 1), (couples,), 0, 1 << 20) % (slack + 1)
    tallies = tallies.at[1:1 + 2 * couples:2].set(source_of - passed).at[2:2 + 2 * couples:2].set(taker + passed)
    return tallies[jax.random.permutation(jax.random.fold_in(key, 2), count)]


def noise(own_key, shape, deviation, most, split=(), kind=jnp.bfloat16):
    drawn = jax.random.normal(own_key, shape, jnp.float32) * deviation
    if len(split) > 0:
        drawn = block_scale(own_key, shape, split, -0.22, 0.18) * drawn
    return jnp.clip(drawn, min=-most, max=most).astype(kind)


def setup_inputs(seed: int = 0) -> dict:
    arg_keys = jax.random.split(jax.random.key(seed), 4)
    traces = noise(arg_keys[0], (DAYS, CHANNELS, SAMP), 1.0, 6.0, ((0, 8), (1, 64)), jnp.float32)
    counts = ragged(arg_keys[1], N_BLOCK, N_BLOCK * CAP * 3 // 4, CAP, 2).astype(jnp.int32)
    order = jax.random.permutation(arg_keys[2], N_BLOCK).astype(jnp.int32)
    return dict(traces=traces, counts=counts, order=order)


clip_level = 2.5

def whiten(traces, counts):
    days, chans, samples = traces.shape
    pieces = traces.reshape(days, chans, samples // SEG, SEG)
    centered = pieces - lax.optimization_barrier(jnp.mean(pieces, axis=3, keepdims=True))
    rms = jnp.sqrt(lax.optimization_barrier(jnp.mean(centered * centered, axis=3, keepdims=True)) + 1e-05)
    slot = jnp.arange(chans, dtype=jnp.int32)
    block_of = (slot // CAP).astype(jnp.int32)
    live = (slot % CAP < counts[block_of]).astype(jnp.float32)
    white = jnp.clip(centered / rms, -clip_level, clip_level) * live[None, :, None, None]
    return white.astype(jnp.bfloat16)

def correlate(own_rows, owner_rows):
    segments = own_rows.shape[1]
    padded = jnp.pad(owner_rows, ((0, 0), (0, 0), (HALF, HALF)))
    total = jnp.zeros((owner_rows.shape[0], LAGS, own_rows.shape[0]), jnp.float32)
    for segment in range(segments):
        for part in range(SEG // TIME_BLOCK):
            begin = part * TIME_BLOCK
            window = padded[:, segment, begin:begin + TIME_BLOCK + 2 * HALF]
            shifted = jnp.stack([window[:, lag:lag + TIME_BLOCK] for lag in range(LAGS)], 0).astype(jnp.float32)
            local = own_rows[:, segment, begin:begin + TIME_BLOCK].astype(jnp.float32)
            total = total + jnp.einsum('ljt,ct->jlc', shifted, local)
    return total

def reference(traces, counts, order):
    white = whiten(traces, counts)
    scale = float(DAYS * SAMP) ** (-0.5)
    results = []
    for step in range(STEPS):
        owner = order[step].astype(jnp.int32)

        def add_day(day, total):
            day_white = lax.dynamic_index_in_dim(white, day, 0, keepdims=False)
            owner_rows = lax.dynamic_slice_in_dim(day_white, (owner * CAP).astype(jnp.int32), CAP, 0)
            return total + correlate(day_white, owner_rows)
        start = jnp.zeros((CAP, LAGS, CHANNELS), jnp.float32)
        total = lax.fori_loop(0, DAYS, add_day, start)
        results.append(total * scale)
    return jnp.stack(results, 0)
```

```python
import jax
import jax.numpy as jnp
from jax import lax
from jax.experimental import pallas as pl
from jax.experimental.pallas import tpu as pltpu
from jax.sharding import PartitionSpec as P

MESH = pl.DeviceIdType.MESH

SEG = 2400
LAGS = 61
STEPS = 3
HALF = 30
CAP = 64
CLIP = 2.5
DAYS = 8
NZ = 16
PLANE = 4
SHARE = 8
FOLD = 10
WIDE = 2 * FOLD * 128
K = 2432
OWN_SHIFTS = 8
OWNER_SHIFTS = 8
ROWS = OWNER_SHIFTS * STEPS * SHARE
COLS = OWN_SHIFTS * CAP
PARTS = 15
PER = 4
F32 = jnp.float32
BF16 = jnp.bfloat16


def unfold(tiles):
    top, low = [], []
    for i in range(FOLD):
        tile = tiles[i].astype(F32)
        top.append(tile[0:8])
        low.append(tile[8:16])
    return jnp.concatenate(top + low, axis=1)[:, :K]


def kernel(order, counts, x_ref, out_ref, wide, gathered, first, chosen, along, full, shifted, acc,
           first_s, first_r, own_s, own_r, spread_s, spread_r, part_s, part_r, plane_s, plane_r):
    b = lax.axis_index("block")
    d = lax.axis_index("day")
    z = b // PLANE
    p = b % PLANE
    here = p * DAYS + d

    barrier = pltpu.get_barrier_semaphore()

    def greet_plane(k, _):
        m = (here + k) % (PLANE * DAYS)
        pl.semaphore_signal(barrier, 1, device_id=(z * PLANE + m // DAYS, m % DAYS), device_id_type=MESH)
        return 0

    def greet_line(k, _):
        pl.semaphore_signal(barrier, 1, device_id=(((z + k) % NZ) * PLANE + p, d), device_id_type=MESH)
        return 0

    lax.fori_loop(1, NZ, greet_line, 0)
    lax.fori_loop(1, PLANE * DAYS, greet_plane, 0)

    x = x_ref[0]
    centered = x - jnp.sum(x, axis=1, keepdims=True) * (1.0 / SEG)
    rms = jnp.sqrt(jnp.sum(centered * centered, axis=1, keepdims=True) * (1.0 / SEG) + 1e-05)
    live = (lax.broadcasted_iota(jnp.int32, (CAP, 1), 0) < counts[b]).astype(F32)
    wide[:, K - 128:] = jnp.zeros((CAP, WIDE - K + 128), F32)
    wide[:, :SEG] = jnp.clip(centered * (1.0 / rms), -CLIP, CLIP) * live
    for g in range(DAYS):
        for i in range(FOLD):
            top = wide[8 * g:8 * g + 8, 128 * i:128 * i + 128]
            low = wide[8 * g:8 * g + 8, 128 * (i + FOLD):128 * (i + FOLD) + 128]
            gathered[d, g, i] = jnp.concatenate([top, low], axis=0).astype(BF16)

    pl.semaphore_wait(barrier, NZ - 1 + PLANE * DAYS - 1)

    to_p = d // 2
    slot = p * 2 + d % 2

    def first_copy(k):
        to_d = (d + k) % DAYS
        return pltpu.make_async_remote_copy(
            gathered.at[d, to_d], first.at[slot], first_s.at[k], first_r.at[slot],
            device_id=(z * PLANE + to_p, to_d), device_id_type=MESH)

    for k in range(DAYS):
        if k == 0:
            @pl.when(p != to_p)
            def _():
                first_copy(0).start()

            @pl.when(p == to_p)
            def _():
                first[slot] = gathered[d, d]
        else:
            first_copy(k).start()

    def own_copy(k):
        return pltpu.make_async_remote_copy(
            gathered.at[d], gathered.at[d], own_s.at[k], own_r.at[d],
            device_id=(b, (d + k) % DAYS), device_id_type=MESH)

    def own_arrival(day):
        return pltpu.make_async_remote_copy(
            gathered.at[day], gathered.at[day], own_s.at[0], own_r.at[day],
            device_id=(b, day), device_id_type=MESH)

    for j in range(2 * PLANE):
        @pl.when(jnp.logical_or(p != to_p, slot != j))
        def _():
            pltpu.make_async_remote_copy(
                first.at[j], first.at[j], first_s.at[0], first_r.at[j],
                device_id=(b, d), device_id_type=MESH).wait_recv()

    for s in range(STEPS):
        for half in range(2):
            at = (s * 2 + half) * FOLD
            chosen[at:at + FOLD] = first[(order[s] % PLANE) * 2 + half]

    def spread_copy(k):
        to_z = (z + k) % NZ
        return to_z, pltpu.make_async_remote_copy(
            chosen.at[pl.ds(jnp.minimum(to_z, PARTS - 1) * PER, PER)], along.at[z], spread_s.at[k], spread_r.at[z],
            device_id=(to_z * PLANE + p, d), device_id_type=MESH)

    order_of_hops = [8, 7, 9, 6, 10, 5, 11, 4, 12, 3, 13, 2, 14, 1, 15]
    for k in order_of_hops:
        to_z, copy = spread_copy(k)

        @pl.when(to_z < PARTS)
        def _():
            copy.start()
    for k in range(1, DAYS):
        own_copy(k).start()

    def shifts_of_day(day):
        def group(g, _):
            rows = jnp.concatenate([unfold(gathered[day, 2 * g]), unfold(gathered[day, 2 * g + 1])], axis=0)
            for r in range(OWN_SHIFTS):
                rolled = rows if r == 0 else pltpu.roll(rows, r, 1)
                at = pl.multiple_of(r * CAP + g * 16, 16)
                shifted[day, pl.ds(at, 16), :] = rolled.astype(BF16)
            return 0
        lax.fori_loop(0, CAP // 16, group, 0)

    shifts_of_day(d)

    @pl.when(z < PARTS)
    def _():
        along[z] = chosen[pl.ds(z * PER, PER)]
        for k in range(1, NZ):
            src = (z + k) % NZ
            pltpu.make_async_remote_copy(
                along.at[src], along.at[src], spread_s.at[0], spread_r.at[src],
                device_id=(b, d), device_id_type=MESH).wait_recv()
        full[p, pl.ds(z * PER, PER)] = along[order[z // (PARTS // STEPS)] // PLANE]

    def part_copy(k):
        at = pl.ds(jnp.minimum(z, PARTS - 1) * PER, PER)
        return pltpu.make_async_remote_copy(
            full.at[p, at], full.at[p, at], part_s.at[k], part_r.at[jnp.minimum(z, PARTS - 1)],
            device_id=(((z + k) % NZ) * PLANE + p, d), device_id_type=MESH)

    @pl.when(z < PARTS)
    def _():
        for k in order_of_hops:
            part_copy(k).start()

    def more_days(k, _):
        day = (d + k) % DAYS
        own_arrival(day).wait_recv()
        shifts_of_day(day)
        return 0

    lax.fori_loop(1, 4, more_days, 0)

    for src in range(PARTS):
        @pl.when(src != z)
        def _():
            at = pl.ds(src * PER, PER)
            pltpu.make_async_remote_copy(
                full.at[p, at], full.at[p, at], part_s.at[0], part_r.at[src],
                device_id=(b, d), device_id_type=MESH).wait_recv()

    def plane_copy(k):
        return pltpu.make_async_remote_copy(
            full.at[p], full.at[p], plane_s.at[k], plane_r.at[p],
            device_id=(z * PLANE + (p + k) % PLANE, d), device_id_type=MESH)

    for k in (2, 1, 3):
        plane_copy(k).start()

    lax.fori_loop(4, DAYS, more_days, 0)

    acc[...] = jnp.zeros_like(acc)

    def day_sums(day):
        source, half = day // 2, day % 2
        rows = jnp.concatenate(
            [unfold(full[source, pl.ds(s * 2 * FOLD + half * FOLD, FOLD)]) for s in range(STEPS)], axis=0)
        left = jnp.concatenate(
            [pltpu.roll(rows, (HALF - OWN_SHIFTS * q) % K, 1) for q in range(OWNER_SHIFTS)], axis=0).astype(BF16)
        acc[...] += lax.dot_general(left, shifted[day], (((1,), (1,)), ((), ())), preferred_element_type=F32)

    def two_days(k, _):
        source = (p + k) % PLANE

        @pl.when(k > 0)
        def _():
            pltpu.make_async_remote_copy(
                full.at[source], full.at[source], plane_s.at[0], plane_r.at[source],
                device_id=(b, d), device_id_type=MESH).wait_recv()

        def one(half, _):
            day_sums(source * 2 + half)
            return 0
        lax.fori_loop(0, 2, one, 0)
        return 0

    lax.fori_loop(0, PLANE, two_days, 0)
    out_ref[...] = acc[...] * (float(DAYS * SEG) ** -0.5)

    @pl.when(p != to_p)
    def _():
        first_copy(0).wait_send()
    for k in range(1, DAYS):
        first_copy(k).wait_send()
        own_copy(k).wait_send()
    for k in order_of_hops:
        to_z, copy = spread_copy(k)

        @pl.when(to_z < PARTS)
        def _():
            copy.wait_send()

    @pl.when(z < PARTS)
    def _():
        for k in order_of_hops:
            part_copy(k).wait_send()
    for k in (2, 1, 3):
        plane_copy(k).wait_send()


def per_device(traces, counts, order):
    dma = pltpu.SemaphoreType.DMA
    tile = (16, 128)
    raw = pl.pallas_call(
        kernel,
        out_shape=jax.ShapeDtypeStruct((ROWS, COLS), F32),
        in_specs=[pl.BlockSpec(memory_space=pltpu.SMEM), pl.BlockSpec(memory_space=pltpu.SMEM),
                  pl.BlockSpec(memory_space=pltpu.VMEM)],
        out_specs=pl.BlockSpec(memory_space=pltpu.VMEM),
        scratch_shapes=[
            pltpu.VMEM((CAP, WIDE), F32),
            pltpu.VMEM((DAYS, DAYS, FOLD) + tile, BF16),
            pltpu.VMEM((2 * PLANE, FOLD) + tile, BF16),
            pltpu.VMEM((PARTS * PER,) + tile, BF16),
            pltpu.VMEM((NZ, PER) + tile, BF16),
            pltpu.VMEM((PLANE, PARTS * PER) + tile, BF16),
            pltpu.VMEM((DAYS, COLS, K), BF16),
            pltpu.VMEM((ROWS, COLS), F32),
            dma((DAYS,)), dma((2 * PLANE,)), dma((DAYS,)), dma((DAYS,)),
            dma((NZ,)), dma((NZ,)), dma((NZ,)), dma((NZ,)), dma((PLANE,)), dma((PLANE,)),
        ],
        compiler_params=pltpu.CompilerParams(
            collective_id=0, has_side_effects=True, vmem_limit_bytes=48 << 20),
        cost_estimate=pl.CostEstimate(flops=2 * ROWS * COLS * K * DAYS, bytes_accessed=1 << 20, transcendentals=0),
        name="correlate",
    )(order, counts, traces)
    parts = raw.reshape(OWNER_SHIFTS, STEPS, SHARE, OWN_SHIFTS, CAP)
    lags = parts.transpose(1, 2, 0, 3, 4).reshape(STEPS, SHARE, OWNER_SHIFTS * OWN_SHIFTS, CAP)
    return lags[:, :, :LAGS]


def solution(mesh):
    return jax.shard_map(
        per_device, mesh=mesh, in_specs=(P("day", "block", None), P(), P()),
        out_specs=P(None, "day", None, "block"), check_vma=False)
```

```python
import jax
import jax.numpy as jnp
from jax import lax
from jax.experimental import pallas as pl
from jax.experimental.pallas import tpu as pltpu
from jax.sharding import PartitionSpec as P

MESH = pl.DeviceIdType.MESH

SEG = 2400
LAGS = 61
STEPS = 3
HALF = 30
CAP = 64
CLIP = 2.5
DAYS = 8
NZ = 16
NX = 4
PLANE = 4
TILES = 19
K = TILES * 128
SHARE = 16
OWN_SHIFTS = 8
OWNER_SHIFTS = 8
ROWS = OWNER_SHIFTS * STEPS * SHARE // 2
COLS = OWN_SHIFTS * CAP
CLASSES = 4
PER = 5
GROUP = STEPS * PER
F32 = jnp.float32
BF16 = jnp.bfloat16


def kernel(order_hbm, counts_hbm, x_hbm, out_ref, order, counts, x_ref, wide, gathered, first, far, full,
           shifted, acc, outgoing, incoming, load, first_s, first_r, own_s, own_r, far_s, far_r, full_r,
           line_s, core_s, sum_s, sum_r):
    b = lax.axis_index("block")
    d = lax.axis_index("day")
    z = b // PLANE
    p = b % PLANE
    x = d // 2
    yh = d % 2
    mine = z % CLASSES
    two = 2 - 4 * (p % 2)
    two_x = 2 - 4 * (x % 2)
    q = (p + 2) % PLANE
    mate = p + 1 - 2 * (p % 2)

    def at_device(hop, plane, day):
        return ((z + hop + NZ) % NZ) * PLANE + plane, day

    def day_at(k):
        return ((x + k) % NX) * 2 + yh

    loads = [pltpu.make_async_copy(x_hbm.at[0], x_ref, load.at[0]),
             pltpu.make_async_copy(order_hbm, order, load.at[1]),
             pltpu.make_async_copy(counts_hbm, counts, load.at[2])]
    for copy in loads:
        copy.start()

    barrier = pltpu.get_barrier_semaphore()

    def greet(device):
        pl.semaphore_signal(barrier, 1, device_id=device, device_id_type=MESH)

    spots = ((two, q), (two, p), (1, q), (-1, q), (1, p), (-1, p), (0, q))
    for j in (2, 1, 3):
        greet(at_device(CLASSES * j, p, d))
    for i, hop in enumerate((-two, -1, 1, 0)):
        for plane in range(PLANE):
            device = at_device(hop, plane, p * 2 + yh)
            if i < 3:
                greet(device)
            else:
                @pl.when(jnp.logical_or(plane != p, p != x))
                def _():
                    greet(device)
    for hop, plane in spots:
        greet(at_device(-hop, plane, d))
    for k in range(1, NX):
        greet(at_device(0, p, day_at(k)))
    greet(at_device(0, mate, d))
    greet(at_device(0, p, x * 2 + 1 - yh))
    for copy in loads:
        copy.wait()

    rows = x_ref[...]
    centered = rows - jnp.sum(rows, axis=1, keepdims=True) * (1.0 / SEG)
    rms = jnp.sqrt(jnp.sum(centered * centered, axis=1, keepdims=True) * (1.0 / SEG) + 1e-05)
    live = (lax.broadcasted_iota(jnp.int32, (CAP, 1), 0) < counts[b]).astype(F32)
    wide[:, K - 128:] = jnp.zeros((CAP, 128), F32)
    wide[:, :SEG] = jnp.clip(centered * (1.0 / rms), -CLIP, CLIP) * live
    for g in range(NX):
        for i in range(TILES):
            gathered[x, g, i] = wide[16 * g:16 * g + 16, 128 * i:128 * i + 128].astype(BF16)
        gathered[x, g, TILES] = jnp.zeros((16, 128), BF16)

    pl.semaphore_wait(barrier, 31 - (p == x).astype(jnp.int32))

    hops = (0, 1, -1, two_x)

    def first_copy(i, k):
        to_class = (z + hops[i] + NZ) % CLASSES
        return pltpu.make_async_remote_copy(
            gathered.at[x, (x + k) % NX, pl.ds(to_class * PER, PER)], first.at[i * PLANE + p],
            first_s.at[i * NX + k], first_r.at[i * PLANE + p],
            device_id=at_device(hops[i], x, day_at(k)), device_id_type=MESH)

    @pl.when(p != x)
    def _():
        first_copy(0, 0).start()

    @pl.when(p == x)
    def _():
        first[p] = gathered[x, x, pl.ds(mine * PER, PER)]

    firsts = [(i, k) for k in (2, 1, 3, 0) for i in (3, 1, 2, 0) if i or k]
    for i, k in firsts:
        first_copy(i, k).start()

    def own_copy(k):
        return pltpu.make_async_remote_copy(
            gathered.at[x], gathered.at[x], own_s.at[k], own_r.at[x],
            device_id=at_device(0, p, day_at(k)), device_id_type=MESH)

    def shifts_of_day(day):
        def group(g, _):
            rows = jnp.concatenate([gathered[day, g, i].astype(F32) for i in range(TILES)], axis=1)
            for r in range(OWN_SHIFTS):
                rolled = rows if r == 0 else pltpu.roll(rows, r, 1)
                at = pl.multiple_of(r * CAP + g * 16, 16)
                shifted[day, pl.ds(at, 16), :] = rolled.astype(BF16)
            return 0
        lax.fori_loop(0, CAP // 16, group, 0)

    def own_shifts(k, _):
        day = (x + NX - k) % NX
        pltpu.make_async_remote_copy(
            gathered.at[day], gathered.at[day], own_s.at[k], own_r.at[day],
            device_id=(b, d), device_id_type=MESH).wait_recv()
        shifts_of_day(day)
        return 0

    shifts_of_day(x)
    for j in range(CLASSES * PLANE):
        @pl.when(jnp.logical_or(p != x, p != j))
        def _():
            pltpu.make_async_remote_copy(
                first.at[j], first.at[j], first_s.at[0], first_r.at[j],
                device_id=(b, d), device_id_type=MESH).wait_recv()

    for s in range(STEPS):
        gap = (z - order[s] // PLANE + NZ) % NZ
        came = jnp.where(gap == 1, 1, jnp.where(gap == NZ - 1, 2, jnp.where(gap == (two + NZ) % NZ, 3, 0)))
        far[z // CLASSES, s * PER:(s + 1) * PER] = first[came * PLANE + order[s] % PLANE]

    def far_copy(j):
        return pltpu.make_async_remote_copy(
            far.at[z // CLASSES], far.at[z // CLASSES], far_s.at[j], far_r.at[z // CLASSES],
            device_id=at_device(CLASSES * j, p, d), device_id_type=MESH)

    for j in (2, 1, 3):
        far_copy(j).start()
    for k in (1, 3, 2):
        own_copy(k).start()
    for j in (1, 3, 2):
        src = (z // CLASSES + j) % CLASSES
        pltpu.make_async_remote_copy(
            far.at[src], far.at[src], far_s.at[j], far_r.at[src],
            device_id=(b, d), device_id_type=MESH).wait_recv()
    for s in range(STEPS):
        owner_z = order[s] // PLANE
        gap = (mine - owner_z + NZ) % CLASSES
        step = jnp.where(gap == 3, -1, jnp.where(gap == 2, two, gap))
        sender = (owner_z + step + NZ) % NZ
        full[p, mine, s * PER:(s + 1) * PER] = far[sender // CLASSES, s * PER:(s + 1) * PER]

    def piece(part, cls, sem, to):
        return pltpu.make_async_remote_copy(
            full.at[part, cls], full.at[part, cls], sem, full_r.at[part, cls],
            device_id=to, device_id_type=MESH)

    core = at_device(0, mate, d)

    def spread(j):
        hop, plane = spots[j]
        return piece(p, mine, line_s.at[j], at_device(hop, plane, d))

    def arrival(part, cls):
        piece(part, cls, line_s.at[0], (b, d)).wait_recv()

    def to_core(part, cls):
        piece(part, cls, core_s.at[part, cls], core).start()

    for j in range(len(spots)):
        spread(j).start()
    to_core(p, mine)

    lax.fori_loop(1, NX, own_shifts, 0)

    others = [(z + k + NZ) % CLASSES for k in (1, 3, 2)]
    arrival(q, mine)
    to_core(q, mine)
    for cls in others:
        arrival(p, cls)
        to_core(p, cls)
    for cls in others:
        arrival(q, cls)
        to_core(q, cls)

    acc[...] = jnp.zeros_like(acc)

    def owner_rows(day):
        theirs, ours = [], []
        for s in range(STEPS):
            top, low = [], []
            for t in range(TILES):
                tile = full[day, t // PER, s * PER + t % PER].astype(F32)
                top.append(tile[0:8])
                low.append(tile[8:16])
            top = jnp.concatenate(top, axis=1)
            low = jnp.concatenate(low, axis=1)
            theirs.append(jnp.where(yh == 0, low, top))
            ours.append(jnp.where(yh == 0, top, low))
        return jnp.concatenate(theirs, axis=0), jnp.concatenate(ours, axis=0)

    def add_sums(half, day, rows):
        left = jnp.concatenate(
            [pltpu.roll(rows, (HALF - OWN_SHIFTS * n) % K, 1) for n in range(OWNER_SHIFTS)], axis=0).astype(BF16)
        acc[half] += lax.dot_general(left, shifted[day], (((1,), (1,)), ((), ())), preferred_element_type=F32)

    def whole_day(day):
        theirs, ours = owner_rows(day)
        add_sums(0, day, theirs)
        add_sums(1, day, ours)

    def two_days(k, _):
        whole_day((p + 2 * k) % PLANE)
        return 0

    lax.fori_loop(0, 2, two_days, 0)
    for cls in range(CLASSES):
        arrival(mate, cls)
    whole_day(mate)
    last = (mate + 2) % PLANE
    for cls in range(CLASSES):
        arrival(last, cls)
    theirs, ours = owner_rows(last)
    add_sums(0, last, theirs)
    outgoing[...] = acc[0].astype(BF16)

    def sum_copy():
        return pltpu.make_async_remote_copy(
            outgoing, incoming, sum_s, sum_r, device_id=at_device(0, p, x * 2 + 1 - yh), device_id_type=MESH)

    sum_copy().start()
    add_sums(1, last, ours)

    @pl.when(p != x)
    def _():
        first_copy(0, 0).wait_send()
    for i, k in firsts:
        first_copy(i, k).wait_send()
    for k in range(1, NX):
        own_copy(k).wait_send()
        far_copy(k).wait_send()
    for j in range(len(spots)):
        spread(j).wait_send()
    for part in (p, q):
        for cls in range(CLASSES):
            piece(part, cls, core_s.at[part, cls], core).wait_send()
    sum_copy().wait()
    out_ref[...] = (acc[1] + incoming[...].astype(F32)) * (float(DAYS * SEG) ** -0.5)


def per_device(traces, counts, order):
    dma = pltpu.SemaphoreType.DMA
    tile = (16, 128)
    raw = pl.pallas_call(
        kernel,
        out_shape=jax.ShapeDtypeStruct((ROWS, COLS), F32),
        in_specs=[pl.BlockSpec(memory_space=pltpu.HBM)] * 3,
        out_specs=pl.BlockSpec(memory_space=pltpu.VMEM),
        scratch_shapes=[
            pltpu.SMEM(order.shape, jnp.int32),
            pltpu.SMEM(counts.shape, jnp.int32),
            pltpu.VMEM((CAP, SEG), F32),
            pltpu.VMEM((CAP, K), F32),
            pltpu.VMEM((NX, NX, TILES + 1) + tile, BF16),
            pltpu.VMEM((CLASSES * PLANE, PER) + tile, BF16),
            pltpu.VMEM((CLASSES, GROUP) + tile, BF16),
            pltpu.VMEM((PLANE, CLASSES, GROUP) + tile, BF16),
            pltpu.VMEM((NX, COLS, K), BF16),
            pltpu.VMEM((2, ROWS, COLS), F32),
            pltpu.VMEM((ROWS, COLS), BF16),
            pltpu.VMEM((ROWS, COLS), BF16),
            dma((3,)), dma((CLASSES * NX,)), dma((CLASSES * PLANE,)), dma((NX,)), dma((NX,)),
            dma((CLASSES,)), dma((CLASSES,)), dma((PLANE, CLASSES)),
            dma((7,)), dma((PLANE, CLASSES)), dma, dma,
        ],
        compiler_params=pltpu.CompilerParams(
            collective_id=0, has_side_effects=True, vmem_limit_bytes=63 << 20),
        cost_estimate=pl.CostEstimate(flops=2 * ROWS * COLS * K * DAYS, bytes_accessed=1 << 20, transcendentals=0),
        name="correlate",
    )(order, counts, traces)
    parts = raw.reshape(OWNER_SHIFTS, STEPS, SHARE // 2, OWN_SHIFTS, CAP)
    lags = parts.transpose(1, 2, 0, 3, 4).reshape(STEPS, SHARE // 2, OWNER_SHIFTS * OWN_SHIFTS, CAP)
    return lags[:, :, :LAGS]


def solution(mesh):
    return jax.shard_map(
        per_device, mesh=mesh, in_specs=(P("day", "block", None), P(), P()),
        out_specs=P(None, "day", None, "block"), check_vma=False)
```

```python
import jax
import jax.numpy as jnp
from jax import lax
from jax.experimental import pallas as pl
from jax.experimental.pallas import tpu as pltpu
from jax.sharding import PartitionSpec as P

MESH = pl.DeviceIdType.MESH

SEG = 2400
LAGS = 61
STEPS = 3
HALF = 30
CAP = 64
CLIP = 2.5
DAYS = 8
NZ = 16
NX = 4
PLANE = 4
TILES = 19
K = TILES * 128
SHARE = 16
OWN_SHIFTS = 4
OWNER_SHIFTS = 16
ROWS = OWNER_SHIFTS * SHARE // 2
COLS = OWN_SHIFTS * CAP
CLASSES = 4
PER = 5
F32 = jnp.float32
BF16 = jnp.bfloat16


def kernel(order_hbm, counts_hbm, x_hbm, out_ref, order, counts, x_ref, wide, gathered, first, far_0, far_1, far_2, full,
           shifted, acc, outgoing, incoming, load, first_s, first_r, own_s, own_r, far_s, far_r, full_r,
           line_s, core_s, core_r, sum_s, sum_r):
    far = (far_0, far_1, far_2)
    b = lax.axis_index("block")
    d = lax.axis_index("day")
    z = b // PLANE
    p = b % PLANE
    x = d // 2
    yh = d % 2
    mine = z % CLASSES
    two = 2 - 4 * (p % 2)
    two_x = 2 - 4 * (x % 2)
    q = (p + 2) % PLANE
    mate = p + 1 - 2 * (p % 2)

    def at_device(hop, plane, day):
        return ((z + hop + NZ) % NZ) * PLANE + plane, day

    def day_at(k):
        return ((x + k) % NX) * 2 + yh

    loads = [pltpu.make_async_copy(x_hbm.at[0], x_ref, load.at[0]),
             pltpu.make_async_copy(order_hbm, order, load.at[1]),
             pltpu.make_async_copy(counts_hbm, counts, load.at[2])]
    for copy in loads:
        copy.start()

    barrier = pltpu.get_barrier_semaphore()

    def greet(device):
        pl.semaphore_signal(barrier, 1, device_id=device, device_id_type=MESH)

    spots = ((two, q), (two, p), (1, q), (-1, q), (1, p), (-1, p), (0, q))
    for j in (2, 1, 3):
        greet(at_device(CLASSES * j, p, d))
    for i, hop in enumerate((-two, -1, 1, 0)):
        for plane in range(PLANE):
            device = at_device(hop, plane, p * 2 + yh)
            if i < 3:
                greet(device)
            else:
                @pl.when(jnp.logical_or(plane != p, p != x))
                def _():
                    greet(device)
    for hop, plane in spots:
        greet(at_device(-hop, plane, d))
    for k in range(1, NX):
        greet(at_device(0, p, day_at(k)))
    greet(at_device(0, mate, d))
    greet(at_device(0, p, x * 2 + 1 - yh))
    for copy in loads:
        copy.wait()

    rows = x_ref[...]
    centered = rows - jnp.sum(rows, axis=1, keepdims=True) * (1.0 / SEG)
    rms = jnp.sqrt(jnp.sum(centered * centered, axis=1, keepdims=True) * (1.0 / SEG) + 1e-05)
    live = (lax.broadcasted_iota(jnp.int32, (CAP, 1), 0) < counts[b]).astype(F32)
    wide[:, K - 128:] = jnp.zeros((CAP, 128), F32)
    wide[:, :SEG] = jnp.clip(centered * (1.0 / rms), -CLIP, CLIP) * live
    for g in range(NX):
        for i in range(TILES):
            gathered[x, g, i] = wide[16 * g:16 * g + 16, 128 * i:128 * i + 128].astype(BF16)
        gathered[x, g, TILES] = jnp.zeros((16, 128), BF16)

    pl.semaphore_wait(barrier, 31 - (p == x).astype(jnp.int32))

    hops = (0, 1, -1, two_x)

    def first_copy(i, k):
        to_class = (z + hops[i] + NZ) % CLASSES
        return pltpu.make_async_remote_copy(
            gathered.at[x, (x + k) % NX, pl.ds(to_class * PER, PER)], first.at[i * PLANE + p],
            first_s.at[i * NX + k], first_r.at[i * PLANE + p],
            device_id=at_device(hops[i], x, day_at(k)), device_id_type=MESH)

    @pl.when(p != x)
    def _():
        first_copy(0, 0).start()

    @pl.when(p == x)
    def _():
        first[p] = gathered[x, x, pl.ds(mine * PER, PER)]

    firsts = [(i, k) for k in (2, 1, 3, 0) for i in (3, 1, 2, 0) if i or k]
    for i, k in firsts:
        first_copy(i, k).start()

    def own_copy(k):
        return pltpu.make_async_remote_copy(
            gathered.at[x], gathered.at[x], own_s.at[k], own_r.at[x],
            device_id=at_device(0, p, day_at(k)), device_id_type=MESH)

    for k in (1, 3, 2):
        own_copy(k).start()

    def shifts_of_day(day):
        def group(g, _):
            rows = jnp.concatenate([gathered[day, g, i] for i in range(TILES)], axis=1)
            for r in range(OWN_SHIFTS):
                rolled = rows if r == 0 else pltpu.roll(rows, r, 1)
                at = pl.multiple_of(r * CAP + g * 16, 16)
                shifted[day, pl.ds(at, 16), :] = rolled
            return 0
        lax.fori_loop(0, CAP // 16, group, 0)

    def own_shifts(k, _):
        day = (x + NX - k) % NX
        pltpu.make_async_remote_copy(
            gathered.at[day], gathered.at[day], own_s.at[k], own_r.at[day],
            device_id=(b, d), device_id_type=MESH).wait_recv()
        shifts_of_day(day)
        return 0

    shifts_of_day(x)
    for j in range(CLASSES * PLANE):
        @pl.when(jnp.logical_or(p != x, p != j))
        def _():
            pltpu.make_async_remote_copy(
                first.at[j], first.at[j], first_s.at[0], first_r.at[j],
                device_id=(b, d), device_id_type=MESH).wait_recv()

    def far_copy(s, j):
        return pltpu.make_async_remote_copy(
            far[s].at[z // CLASSES], far[s].at[z // CLASSES], far_s.at[s, j], far_r.at[s, z // CLASSES],
            device_id=at_device(CLASSES * j, p, d), device_id_type=MESH)

    for s in range(STEPS):
        gap = (z - order[s] // PLANE + NZ) % NZ
        came = jnp.where(gap == 1, 1, jnp.where(gap == NZ - 1, 2, jnp.where(gap == (two + NZ) % NZ, 3, 0)))
        far[s][z // CLASSES] = first[came * PLANE + order[s] % PLANE]
        for j in (2, 1, 3):
            far_copy(s, j).start()

    def piece(s, part, cls, sem, to):
        return pltpu.make_async_remote_copy(
            full.at[s, part, cls], full.at[s, part, cls], sem, full_r.at[s * PLANE + part, cls],
            device_id=to, device_id_type=MESH)

    core = at_device(0, mate, d)

    def spread(s, j):
        hop, plane = spots[j]
        return piece(s, p, mine, line_s.at[s, j], at_device(hop, plane, d))

    def arrival(s, part, cls):
        piece(s, part, cls, line_s.at[0, 0], (b, d)).wait_recv()

    def core_copy(s, part):
        return pltpu.make_async_remote_copy(
            full.at[s, part], full.at[s, part], core_s.at[s, part], core_r.at[s, part],
            device_id=core, device_id_type=MESH)

    others = [(z + k + NZ) % CLASSES for k in (1, 3, 2)]

    def open_owner(s):
        for j in (1, 3, 2):
            src = (z // CLASSES + j) % CLASSES
            pltpu.make_async_remote_copy(
                far[s].at[src], far[s].at[src], far_s.at[s, j], far_r.at[s, src],
                device_id=(b, d), device_id_type=MESH).wait_recv()
        owner_z = order[s] // PLANE
        gap = (mine - owner_z + NZ) % CLASSES
        step = jnp.where(gap == 3, -1, jnp.where(gap == 2, two, gap))
        sender = (owner_z + step + NZ) % NZ
        full[s, p, mine] = far[s][sender // CLASSES]
        for j in range(len(spots)):
            spread(s, j).start()

    def pass_on(s):
        for cls in others:
            arrival(s, p, cls)
        core_copy(s, p).start()
        arrival(s, q, mine)
        for cls in others:
            arrival(s, q, cls)
        core_copy(s, q).start()

    def from_core(s):
        for part in (mate, (mate + 2) % PLANE):
            core_copy(s, part).wait_recv()

    def add_days(s, part):
        def one(k, _):
            day = (part + 2 * k) % PLANE
            rows = jnp.concatenate(
                [full[s, day, t // PER, t % PER] for t in range(TILES)], axis=1)
            left = jnp.concatenate(
                [pltpu.roll(rows, (HALF - OWN_SHIFTS * n) % K, 1) for n in range(OWNER_SHIFTS)], axis=0)
            sums = lax.dot_general(left, shifted[day], (((1,), (1,)), ((), ())), preferred_element_type=F32)
            acc[s] += sums
            return 0
        lax.fori_loop(0, 2, one, 0)

    def sum_copy(s):
        return pltpu.make_async_remote_copy(
            outgoing.at[s], incoming.at[s], sum_s.at[s], sum_r.at[s],
            device_id=at_device(0, p, x * 2 + 1 - yh), device_id_type=MESH)

    def halves(s):
        whole = acc[s].reshape(OWNER_SHIFTS, 2, SHARE // 2, COLS)
        return whole[:, 0].reshape(ROWS, COLS), whole[:, 1].reshape(ROWS, COLS)

    def to_partner(s):
        top, low = halves(s)
        outgoing[s] = jnp.where(yh == 0, low, top).astype(BF16)
        sum_copy(s).start()

    def finish(s):
        sum_copy(s).wait_recv()
        top, low = halves(s)
        out_ref[s] = (jnp.where(yh == 0, top, low) + incoming[s].astype(F32)) * (float(DAYS * SEG) ** -0.5)

    acc[...] = jnp.zeros_like(acc)
    open_owner(0)
    open_owner(1)
    own_shifts(1, 0)
    open_owner(2)
    lax.fori_loop(2, NX, own_shifts, 0)
    pass_on(0)
    add_days(0, p)
    pass_on(1)
    from_core(0)
    add_days(0, mate)
    to_partner(0)
    add_days(1, p)
    pass_on(2)
    from_core(1)
    add_days(1, mate)
    to_partner(1)
    add_days(2, p)
    from_core(2)
    add_days(2, mate)
    to_partner(2)

    @pl.when(p != x)
    def _():
        first_copy(0, 0).wait_send()
    for i, k in firsts:
        first_copy(i, k).wait_send()
    for k in range(1, NX):
        own_copy(k).wait_send()
    for s in range(STEPS):
        for k in range(1, NX):
            far_copy(s, k).wait_send()
        for j in range(len(spots)):
            spread(s, j).wait_send()
        for part in (p, q):
            core_copy(s, part).wait_send()
    for s in range(STEPS):
        finish(s)
        sum_copy(s).wait_send()


def per_device(traces, counts, order):
    dma = pltpu.SemaphoreType.DMA
    tile = (16, 128)
    raw = pl.pallas_call(
        kernel,
        out_shape=jax.ShapeDtypeStruct((STEPS, ROWS, COLS), F32),
        in_specs=[pl.BlockSpec(memory_space=pltpu.HBM)] * 3,
        out_specs=pl.BlockSpec(memory_space=pltpu.VMEM),
        scratch_shapes=[
            pltpu.SMEM(order.shape, jnp.int32),
            pltpu.SMEM(counts.shape, jnp.int32),
            pltpu.VMEM((CAP, SEG), F32),
            pltpu.VMEM((CAP, K), F32),
            pltpu.VMEM((NX, NX, TILES + 1) + tile, BF16),
            pltpu.VMEM((CLASSES * PLANE, PER) + tile, BF16),
            pltpu.VMEM((CLASSES, PER) + tile, BF16),
            pltpu.VMEM((CLASSES, PER) + tile, BF16),
            pltpu.VMEM((CLASSES, PER) + tile, BF16),
            pltpu.VMEM((STEPS, PLANE, CLASSES, PER) + tile, BF16),
            pltpu.VMEM((NX, COLS, K), BF16),
            pltpu.VMEM((STEPS, 2 * ROWS, COLS), F32),
            pltpu.VMEM((STEPS, ROWS, COLS), BF16),
            pltpu.VMEM((STEPS, ROWS, COLS), BF16),
            dma((3,)), dma((CLASSES * NX,)), dma((CLASSES * PLANE,)), dma((NX,)), dma((NX,)),
            dma((STEPS, CLASSES)), dma((STEPS, CLASSES)), dma((STEPS * PLANE, CLASSES)),
            dma((STEPS, 7)), dma((STEPS, PLANE)), dma((STEPS, PLANE)), dma((STEPS,)), dma((STEPS,)),
        ],
        compiler_params=pltpu.CompilerParams(
            collective_id=0, has_side_effects=True, vmem_limit_bytes=63 << 20),
        cost_estimate=pl.CostEstimate(flops=2 * STEPS * ROWS * COLS * K * DAYS, bytes_accessed=1 << 20, transcendentals=0),
        name="correlate",
    )(order, counts, traces)
    parts = raw.reshape(STEPS, OWNER_SHIFTS, SHARE // 2, OWN_SHIFTS, CAP)
    lags = parts.transpose(0, 2, 1, 3, 4).reshape(STEPS, SHARE // 2, OWNER_SHIFTS * OWN_SHIFTS, CAP)
    return lags[:, :, :LAGS]


def solution(mesh):
    return jax.shard_map(
        per_device, mesh=mesh, in_specs=(P("day", "block", None), P(), P()),
        out_specs=P(None, "day", None, "block"), check_vma=False)
```

```python
import jax
import jax.numpy as jnp
from jax import lax
from jax.experimental import pallas as pl
from jax.experimental.pallas import tpu as pltpu
from jax.sharding import PartitionSpec as P

MESH = pl.DeviceIdType.MESH

SEG = 2400
LAGS = 61
STEPS = 3
HALF = 30
CAP = 64
CLIP = 2.5
DAYS = 8
NZ = 16
NX = 4
PLANE = 4
TILES = 19
K = TILES * 128
SHARE = 16
OWN_SHIFTS = 4
OWNER_SHIFTS = 16
ROWS = OWNER_SHIFTS * SHARE // 2
COLS = OWN_SHIFTS * CAP
CLASSES = 4
PER = 5
F32 = jnp.float32
BF16 = jnp.bfloat16


def kernel(order_hbm, counts_hbm, x_hbm, out_hbm, order, counts, x_ref, wide, gathered, first, far_0, far_1, far_2, full,
           shifted, acc, outgoing, incoming, result, load, first_s, first_r, own_s, own_r, far_s, far_r, full_r,
           line_s, core_s, core_r, sum_s, sum_r, out_s):
    far = (far_0, far_1, far_2)
    b = lax.axis_index("block")
    d = lax.axis_index("day")
    z = b // PLANE
    p = b % PLANE
    x = d // 2
    yh = d % 2
    mine = z % CLASSES
    two = 2 - 4 * (p % 2)
    two_x = 2 - 4 * (x % 2)
    q = (p + 2) % PLANE
    mate = p + 1 - 2 * (p % 2)

    def at_device(hop, plane, day):
        return ((z + hop + NZ) % NZ) * PLANE + plane, day

    def day_at(k):
        return ((x + k) % NX) * 2 + yh

    loads = [pltpu.make_async_copy(
        x_hbm.at[0, pl.ds(pl.multiple_of((x + k) % NX * 16, 16), 16)], x_ref.at[(x + k) % NX], load.at[n])
        for n, k in enumerate((2, 1, 3, 0))]
    loads += [pltpu.make_async_copy(order_hbm, order, load.at[NX]),
              pltpu.make_async_copy(counts_hbm, counts, load.at[NX + 1])]
    barrier = pltpu.get_barrier_semaphore()

    def greet(device):
        pl.semaphore_signal(barrier, 1, device_id=device, device_id_type=MESH)

    spots = ((two, q), (two, p), (1, q), (-1, q), (1, p), (-1, p), (0, q))
    for j in (2, 1, 3):
        greet(at_device(CLASSES * j, p, d))
    for copy in loads:
        copy.start()
    for i, hop in enumerate((-two, -1, 1, 0)):
        for plane in range(PLANE):
            device = at_device(hop, plane, p * 2 + yh)
            if i < 3:
                greet(device)
            else:
                @pl.when(jnp.logical_or(plane != p, p != x))
                def _():
                    greet(device)
    for hop, plane in spots:
        greet(at_device(-hop, plane, d))
    for k in range(1, NX):
        greet(at_device(0, p, day_at(k)))
    greet(at_device(0, mate, d))
    greet(at_device(0, p, x * 2 + 1 - yh))
    for copy in loads[NX:]:
        copy.wait()

    hops = (0, 1, -1, two_x)

    def first_copy(i, k):
        to_class = (z + hops[i] + NZ) % CLASSES
        return pltpu.make_async_remote_copy(
            gathered.at[x, (x + k) % NX, pl.ds(to_class * PER, PER)], first.at[i * PLANE + p],
            first_s.at[i * NX + k], first_r.at[i * PLANE + p],
            device_id=at_device(hops[i], x, day_at(k)), device_id_type=MESH)

    firsts = [(i, k) for k in (2, 1, 3, 0) for i in (3, 1, 2, 0) if i or k]
    for n, k in enumerate((2, 1, 3, 0)):
        g = (x + k) % NX
        loads[n].wait()
        rows = x_ref[g]
        centered = rows - jnp.sum(rows, axis=1, keepdims=True) * (1.0 / SEG)
        rms = jnp.sqrt(jnp.sum(centered * centered, axis=1, keepdims=True) * (1.0 / SEG) + 1e-05)
        live = (16 * g + lax.broadcasted_iota(jnp.int32, (16, 1), 0) < counts[b]).astype(F32)
        wide[:, K - 128:] = jnp.zeros((16, 128), F32)
        wide[:, :SEG] = jnp.clip(centered * (1.0 / rms), -CLIP, CLIP) * live
        for i in range(TILES):
            gathered[x, g, i] = wide[:, 128 * i:128 * i + 128].astype(BF16)
        gathered[x, g, TILES] = jnp.zeros((16, 128), BF16)

    pl.semaphore_wait(barrier, 31 - (p == x).astype(jnp.int32))
    for i, k in firsts:
        first_copy(i, k).start()

    @pl.when(p != x)
    def _():
        first_copy(0, 0).start()

    @pl.when(p == x)
    def _():
        first[p] = gathered[x, x, pl.ds(mine * PER, PER)]

    def own_copy(k):
        return pltpu.make_async_remote_copy(
            gathered.at[x], gathered.at[x], own_s.at[k], own_r.at[x],
            device_id=at_device(0, p, day_at(k)), device_id_type=MESH)

    for k in (1, 3, 2):
        own_copy(k).start()

    def shifts_of_day(day):
        def group(g, _):
            rows = jnp.concatenate([gathered[day, g, i] for i in range(TILES)], axis=1)
            for r in range(OWN_SHIFTS):
                rolled = rows if r == 0 else pltpu.roll(rows, r, 1)
                at = pl.multiple_of(r * CAP + g * 16, 16)
                shifted[day % 2, pl.ds(at, 16), pl.ds(pl.multiple_of(day // 2 * K, 128), K)] = rolled
            return 0
        lax.fori_loop(0, CAP // 16, group, 0)

    def own_shifts(k, _):
        day = (x + NX - k) % NX
        pltpu.make_async_remote_copy(
            gathered.at[day], gathered.at[day], own_s.at[k], own_r.at[day],
            device_id=(b, d), device_id_type=MESH).wait_recv()
        shifts_of_day(day)
        return 0

    shifts_of_day(x)
    for j in range(CLASSES * PLANE):
        @pl.when(jnp.logical_or(p != x, p != j))
        def _():
            pltpu.make_async_remote_copy(
                first.at[j], first.at[j], first_s.at[0], first_r.at[j],
                device_id=(b, d), device_id_type=MESH).wait_recv()

    def far_copy(s, j):
        return pltpu.make_async_remote_copy(
            far[s].at[z // CLASSES], far[s].at[z // CLASSES], far_s.at[s, j], far_r.at[s, z // CLASSES],
            device_id=at_device(CLASSES * j, p, d), device_id_type=MESH)

    for s in range(STEPS):
        gap = (z - order[s] // PLANE + NZ) % NZ
        came = jnp.where(gap == 1, 1, jnp.where(gap == NZ - 1, 2, jnp.where(gap == (two + NZ) % NZ, 3, 0)))
        far[s][z // CLASSES] = first[came * PLANE + order[s] % PLANE]
        for j in (2, 1, 3):
            far_copy(s, j).start()

    def piece(s, part, cls, sem, to):
        return pltpu.make_async_remote_copy(
            full.at[s, part, cls], full.at[s, part, cls], sem, full_r.at[s * PLANE + part, cls],
            device_id=to, device_id_type=MESH)

    core = at_device(0, mate, d)

    def spread(s, j):
        hop, plane = spots[j]
        return piece(s, p, mine, line_s.at[s, j], at_device(hop, plane, d))

    def arrival(s, part, cls):
        piece(s, part, cls, line_s.at[0, 0], (b, d)).wait_recv()

    def core_copy(s, part):
        return pltpu.make_async_remote_copy(
            full.at[s, part], full.at[s, part], core_s.at[s, part], core_r.at[s, part],
            device_id=core, device_id_type=MESH)

    others = [(z + k + NZ) % CLASSES for k in (1, 3, 2)]

    def open_owner(s):
        for j in (1, 3, 2):
            src = (z // CLASSES + j) % CLASSES
            pltpu.make_async_remote_copy(
                far[s].at[src], far[s].at[src], far_s.at[s, j], far_r.at[s, src],
                device_id=(b, d), device_id_type=MESH).wait_recv()
        owner_z = order[s] // PLANE
        gap = (mine - owner_z + NZ) % CLASSES
        step = jnp.where(gap == 3, -1, jnp.where(gap == 2, two, gap))
        sender = (owner_z + step + NZ) % NZ
        full[s, p, mine] = far[s][sender // CLASSES]
        for j in range(len(spots)):
            spread(s, j).start()

    def pass_on(s):
        for cls in others:
            arrival(s, p, cls)
        core_copy(s, p).start()
        arrival(s, q, mine)
        for cls in others:
            arrival(s, q, cls)
        core_copy(s, q).start()

    def from_core(s):
        for part in (mate, (mate + 2) % PLANE):
            core_copy(s, part).wait_recv()

    def add_days(s, part):
        odd = part % 2
        left = []
        for k in range(2):
            rows = jnp.concatenate(
                [full[s, odd + 2 * k, t // PER, t % PER] for t in range(TILES)], axis=1)
            left.append(jnp.concatenate(
                [pltpu.roll(rows, (HALF - OWN_SHIFTS * n) % K, 1) for n in range(OWNER_SHIFTS)], axis=0))
        return lax.dot_general(jnp.concatenate(left, axis=1), shifted[odd], (((1,), (1,)), ((), ())),
                               preferred_element_type=F32)

    def sum_copy(s):
        return pltpu.make_async_remote_copy(
            outgoing.at[s], incoming.at[s], sum_s.at[s], sum_r.at[s],
            device_id=at_device(0, p, x * 2 + 1 - yh), device_id_type=MESH)

    def out_copy(s):
        return pltpu.make_async_copy(result.at[s], out_hbm.at[s], out_s.at[s])

    def halves(s):
        whole = acc[s].reshape(OWNER_SHIFTS, 2, SHARE // 2, COLS)
        return whole[:, 0].reshape(ROWS, COLS), whole[:, 1].reshape(ROWS, COLS)

    def to_partner(s):
        top, low = halves(s)
        outgoing[s] = jnp.where(yh == 0, low, top).astype(BF16)
        sum_copy(s).start()

    def finish(s):
        sum_copy(s).wait_recv()
        top, low = halves(s)
        sums = (jnp.where(yh == 0, top, low) + incoming[s].astype(F32)) * (float(DAYS * SEG) ** -0.5)
        for lag in range(LAGS):
            n, r = lag // OWN_SHIFTS, lag % OWN_SHIFTS
            result[s, lag] = sums[8 * n:8 * n + 8, CAP * r:CAP * r + CAP]
        out_copy(s).start()

    open_owner(0)
    open_owner(1)
    own_shifts(1, 0)
    open_owner(2)
    lax.fori_loop(2, NX, own_shifts, 0)
    pass_on(0)
    acc[0] = add_days(0, p)
    pass_on(1)
    from_core(0)
    acc[0] += add_days(0, mate)
    to_partner(0)
    acc[1] = add_days(1, p)
    pass_on(2)
    from_core(1)
    acc[1] += add_days(1, mate)
    to_partner(1)
    acc[2] = add_days(2, p)
    from_core(2)
    acc[2] += add_days(2, mate)
    to_partner(2)

    @pl.when(p != x)
    def _():
        first_copy(0, 0).wait_send()
    for i, k in firsts:
        first_copy(i, k).wait_send()
    for k in range(1, NX):
        own_copy(k).wait_send()
    for s in range(STEPS):
        for k in range(1, NX):
            far_copy(s, k).wait_send()
        for j in range(len(spots)):
            spread(s, j).wait_send()
        for part in (p, q):
            core_copy(s, part).wait_send()
    for s in range(STEPS):
        finish(s)
        sum_copy(s).wait_send()
    for s in range(STEPS):
        out_copy(s).wait()


def per_device(traces, counts, order):
    dma = pltpu.SemaphoreType.DMA
    tile = (16, 128)
    raw = pl.pallas_call(
        kernel,
        out_shape=jax.ShapeDtypeStruct((STEPS, LAGS, SHARE // 2, CAP), F32),
        in_specs=[pl.BlockSpec(memory_space=pltpu.HBM)] * 3,
        out_specs=pl.BlockSpec(memory_space=pltpu.HBM),
        scratch_shapes=[
            pltpu.SMEM(order.shape, jnp.int32),
            pltpu.SMEM(counts.shape, jnp.int32),
            pltpu.VMEM((NX, 16, SEG), F32),
            pltpu.VMEM((16, K), F32),
            pltpu.VMEM((NX, NX, TILES + 1) + tile, BF16),
            pltpu.VMEM((CLASSES * PLANE, PER) + tile, BF16),
            pltpu.VMEM((CLASSES, PER) + tile, BF16),
            pltpu.VMEM((CLASSES, PER) + tile, BF16),
            pltpu.VMEM((CLASSES, PER) + tile, BF16),
            pltpu.VMEM((STEPS, PLANE, CLASSES, PER) + tile, BF16),
            pltpu.VMEM((2, COLS, 2 * K), BF16),
            pltpu.VMEM((STEPS, 2 * ROWS, COLS), F32),
            pltpu.VMEM((STEPS, ROWS, COLS), BF16),
            pltpu.VMEM((STEPS, ROWS, COLS), BF16),
            pltpu.VMEM((STEPS, LAGS, SHARE // 2, CAP), F32),
            dma((NX + 2,)), dma((CLASSES * NX,)), dma((CLASSES * PLANE,)), dma((NX,)), dma((NX,)),
            dma((STEPS, CLASSES)), dma((STEPS, CLASSES)), dma((STEPS * PLANE, CLASSES)),
            dma((STEPS, 7)), dma((STEPS, PLANE)), dma((STEPS, PLANE)), dma((STEPS,)), dma((STEPS,)), dma((STEPS,)),
        ],
        compiler_params=pltpu.CompilerParams(
            collective_id=0, has_side_effects=True, vmem_limit_bytes=63 << 20),
        cost_estimate=pl.CostEstimate(flops=2 * STEPS * ROWS * COLS * K * DAYS, bytes_accessed=1 << 20, transcendentals=0),
        name="correlate",
    )(order, counts, traces)
    return raw.transpose(0, 2, 1, 3)


def solution(mesh):
    return jax.shard_map(
        per_device, mesh=mesh, in_specs=(P("day", "block", None), P(), P()),
        out_specs=P(None, "day", None, "block"), check_vma=False)
```

```python
import jax
import jax.numpy as jnp
from jax import lax
from jax.experimental import pallas as pl
from jax.experimental.pallas import tpu as pltpu
from jax.sharding import PartitionSpec as P

MESH = pl.DeviceIdType.MESH

SEG = 2400
LAGS = 61
STEPS = 3
HALF = 30
CAP = 64
CLIP = 2.5
DAYS = 8
NZ = 16
NX = 4
PLANE = 4
TILES = 19
K = TILES * 128
SHARE = 16
OWN_SHIFTS = 4
OWNER_SHIFTS = 16
ROWS = OWNER_SHIFTS * SHARE // 2
COLS = OWN_SHIFTS * CAP
CLASSES = 4
PER = 5
F32 = jnp.float32
BF16 = jnp.bfloat16


def kernel(order_hbm, counts_hbm, x_hbm, out_hbm, order, counts, x_ref, wide, gathered, first, far_0, far_1, far_2, full,
           shifted, acc, outgoing, incoming, result, load, first_s, first_r, own_s, own_r, far_s, far_r, full_r,
           line_s, core_s, core_r, sum_s, sum_r, out_s, token):
    far = (far_0, far_1, far_2)
    b = lax.axis_index("block")
    d = lax.axis_index("day")
    z = b // PLANE
    p = b % PLANE
    x = d // 2
    yh = d % 2
    mine = z % CLASSES
    two = 2 - 4 * (p % 2)
    two_x = 2 - 4 * (x % 2)
    q = (p + 2) % PLANE
    mate = p + 1 - 2 * (p % 2)

    def at_device(hop, plane, day):
        return ((z + hop + NZ) % NZ) * PLANE + plane, day

    def day_at(k):
        return ((x + k) % NX) * 2 + yh

    loads = [pltpu.make_async_copy(
        x_hbm.at[0, pl.ds(pl.multiple_of((x + k) % NX * 16, 16), 16)], x_ref.at[(x + k) % NX], load.at[n])
        for n, k in enumerate((2, 1, 3, 0))]
    loads += [pltpu.make_async_copy(order_hbm, order, load.at[NX]),
              pltpu.make_async_copy(counts_hbm, counts, load.at[NX + 1])]
    barrier = pltpu.get_barrier_semaphore()

    def greet(device):
        pl.semaphore_signal(barrier, 1, device_id=device, device_id_type=MESH)

    spots = ((two, q), (two, p), (1, q), (-1, q), (1, p), (-1, p), (0, q))
    for j in (1, 3):
        greet(at_device(CLASSES * j, p, d))
    for copy in loads:
        copy.start()
    for i, hop in enumerate((-two, -1, 1, 0)):
        for plane in range(PLANE):
            device = at_device(hop, plane, p * 2 + yh)
            if i < 3:
                greet(device)
            else:
                @pl.when(jnp.logical_or(plane != p, p != x))
                def _():
                    greet(device)
    for hop, plane in spots:
        greet(at_device(-hop, plane, d))
    for k in range(1, NX):
        greet(at_device(0, p, day_at(k)))
    greet(at_device(0, mate, d))
    greet(at_device(0, p, x * 2 + 1 - yh))
    for copy in loads[NX:]:
        copy.wait()

    hops = (0, 1, -1, two_x)

    def first_copy(i, k):
        to_class = (z + hops[i] + NZ) % CLASSES
        return pltpu.make_async_remote_copy(
            gathered.at[x, (x + k) % NX, pl.ds(to_class * PER, PER)], first.at[i * PLANE + p],
            first_s.at[i * NX + k], first_r.at[i * PLANE + p],
            device_id=at_device(hops[i], x, day_at(k)), device_id_type=MESH)

    firsts = [(i, k) for k in (2, 1, 3, 0) for i in (3, 1, 2, 0) if i or k]
    for n, k in enumerate((2, 1, 3, 0)):
        g = (x + k) % NX
        loads[n].wait()
        rows = x_ref[g]
        centered = rows - jnp.sum(rows, axis=1, keepdims=True) * (1.0 / SEG)
        rms = jnp.sqrt(jnp.sum(centered * centered, axis=1, keepdims=True) * (1.0 / SEG) + 1e-05)
        live = (16 * g + lax.broadcasted_iota(jnp.int32, (16, 1), 0) < counts[b]).astype(F32)
        wide[:, K - 128:] = jnp.zeros((16, 128), F32)
        wide[:, :SEG] = jnp.clip(centered * (1.0 / rms), -CLIP, CLIP) * live
        for i in range(TILES):
            gathered[x, g, i] = wide[:, 128 * i:128 * i + 128].astype(BF16)
        gathered[x, g, TILES] = jnp.zeros((16, 128), BF16)

    pl.semaphore_wait(barrier, 30 - (p == x).astype(jnp.int32))
    pl.semaphore_signal(token, 1, device_id=at_device(-CLASSES, p, d), device_id_type=MESH)
    for i, k in firsts:
        first_copy(i, k).start()

    @pl.when(p != x)
    def _():
        first_copy(0, 0).start()

    @pl.when(p == x)
    def _():
        first[p] = gathered[x, x, pl.ds(mine * PER, PER)]

    def own_copy(k):
        return pltpu.make_async_remote_copy(
            gathered.at[x], gathered.at[x], own_s.at[k], own_r.at[x],
            device_id=at_device(0, p, day_at(k)), device_id_type=MESH)

    for k in (1, 3, 2):
        own_copy(k).start()

    def shifts_of_day(day):
        def group(g, _):
            rows = jnp.concatenate([gathered[day, g, i] for i in range(TILES)], axis=1)
            for r in range(OWN_SHIFTS):
                rolled = rows if r == 0 else pltpu.roll(rows, r, 1)
                at = pl.multiple_of(r * CAP + g * 16, 16)
                shifted[day % 2, pl.ds(at, 16), pl.ds(pl.multiple_of(day // 2 * K, 128), K)] = rolled
            return 0
        lax.fori_loop(0, CAP // 16, group, 0)

    def own_shifts(k, _):
        day = (x + NX - k) % NX
        pltpu.make_async_remote_copy(
            gathered.at[day], gathered.at[day], own_s.at[k], own_r.at[day],
            device_id=(b, d), device_id_type=MESH).wait_recv()
        shifts_of_day(day)
        return 0

    shifts_of_day(x)
    for j in range(CLASSES * PLANE):
        @pl.when(jnp.logical_or(p != x, p != j))
        def _():
            pltpu.make_async_remote_copy(
                first.at[j], first.at[j], first_s.at[0], first_r.at[j],
                device_id=(b, d), device_id_type=MESH).wait_recv()

    def far_copy(s, j):
        return pltpu.make_async_remote_copy(
            far[s].at[z // CLASSES], far[s].at[z // CLASSES], far_s.at[s, j], far_r.at[s, z // CLASSES],
            device_id=at_device(CLASSES * j, p, d), device_id_type=MESH)

    pl.semaphore_wait(token, 1)
    for s in range(STEPS):
        gap = (z - order[s] // PLANE + NZ) % NZ
        came = jnp.where(gap == 1, 1, jnp.where(gap == NZ - 1, 2, jnp.where(gap == (two + NZ) % NZ, 3, 0)))
        far[s][z // CLASSES] = first[came * PLANE + order[s] % PLANE]
        for j in (2, 1, 3):
            far_copy(s, j).start()

    def piece(s, part, cls, sem, to):
        return pltpu.make_async_remote_copy(
            full.at[s, part, cls], full.at[s, part, cls], sem, full_r.at[s * PLANE + part, cls],
            device_id=to, device_id_type=MESH)

    core = at_device(0, mate, d)

    def spread(s, j):
        hop, plane = spots[j]
        return piece(s, p, mine, line_s.at[s, j], at_device(hop, plane, d))

    def arrival(s, part, cls):
        piece(s, part, cls, line_s.at[0, 0], (b, d)).wait_recv()

    def core_copy(s, part):
        return pltpu.make_async_remote_copy(
            full.at[s, part], full.at[s, part], core_s.at[s, part], core_r.at[s, part],
            device_id=core, device_id_type=MESH)

    others = [(z + k + NZ) % CLASSES for k in (1, 3, 2)]

    def open_owner(s):
        for j in (1, 3, 2):
            src = (z // CLASSES + j) % CLASSES
            pltpu.make_async_remote_copy(
                far[s].at[src], far[s].at[src], far_s.at[s, j], far_r.at[s, src],
                device_id=(b, d), device_id_type=MESH).wait_recv()
        owner_z = order[s] // PLANE
        gap = (mine - owner_z + NZ) % CLASSES
        step = jnp.where(gap == 3, -1, jnp.where(gap == 2, two, gap))
        sender = (owner_z + step + NZ) % NZ
        full[s, p, mine] = far[s][sender // CLASSES]
        for j in range(len(spots)):
            spread(s, j).start()

    def pass_on(s):
        for cls in others:
            arrival(s, p, cls)
        core_copy(s, p).start()
        arrival(s, q, mine)
        for cls in others:
            arrival(s, q, cls)
        core_copy(s, q).start()

    def from_core(s):
        for part in (mate, (mate + 2) % PLANE):
            core_copy(s, part).wait_recv()

    def add_days(s, part):
        odd = part % 2
        left = []
        for k in range(2):
            rows = jnp.concatenate(
                [full[s, odd + 2 * k, t // PER, t % PER] for t in range(TILES)], axis=1)
            left.append(jnp.concatenate(
                [pltpu.roll(rows, (HALF - OWN_SHIFTS * n) % K, 1) for n in range(OWNER_SHIFTS)], axis=0))
        return lax.dot_general(jnp.concatenate(left, axis=1), shifted[odd], (((1,), (1,)), ((), ())),
                               preferred_element_type=F32)

    def sum_copy(s):
        return pltpu.make_async_remote_copy(
            outgoing.at[s], incoming.at[s], sum_s.at[s], sum_r.at[s],
            device_id=at_device(0, p, x * 2 + 1 - yh), device_id_type=MESH)

    def out_copy(s):
        return pltpu.make_async_copy(result.at[s], out_hbm.at[s], out_s.at[s])

    def halves(s):
        whole = acc[s].reshape(OWNER_SHIFTS, 2, SHARE // 2, COLS)
        return whole[:, 0].reshape(ROWS, COLS), whole[:, 1].reshape(ROWS, COLS)

    def to_partner(s):
        top, low = halves(s)
        outgoing[s] = jnp.where(yh == 0, low, top).astype(BF16)
        sum_copy(s).start()

    def finish(s):
        sum_copy(s).wait_recv()
        top, low = halves(s)
        sums = (jnp.where(yh == 0, top, low) + incoming[s].astype(F32)) * (float(DAYS * SEG) ** -0.5)
        for lag in range(LAGS):
            n, r = lag // OWN_SHIFTS, lag % OWN_SHIFTS
            result[s, lag] = sums[8 * n:8 * n + 8, CAP * r:CAP * r + CAP]
        out_copy(s).start()

    open_owner(0)
    open_owner(1)
    own_shifts(1, 0)
    open_owner(2)
    lax.fori_loop(2, NX, own_shifts, 0)
    pass_on(0)
    acc[0] = add_days(0, p)
    pass_on(1)
    from_core(0)
    acc[0] += add_days(0, mate)
    to_partner(0)
    acc[1] = add_days(1, p)
    pass_on(2)
    from_core(1)
    acc[1] += add_days(1, mate)
    to_partner(1)
    acc[2] = add_days(2, p)
    from_core(2)
    acc[2] += add_days(2, mate)
    to_partner(2)

    finish(0)

    @pl.when(p != x)
    def _():
        first_copy(0, 0).wait_send()
    for i, k in firsts:
        first_copy(i, k).wait_send()
    for k in range(1, NX):
        own_copy(k).wait_send()
    finish(1)
    for s in range(STEPS):
        for k in range(1, NX):
            far_copy(s, k).wait_send()
        for j in range(len(spots)):
            spread(s, j).wait_send()
        for part in (p, q):
            core_copy(s, part).wait_send()
    finish(2)
    for s in range(STEPS):
        sum_copy(s).wait_send()
        out_copy(s).wait()


def per_device(traces, counts, order):
    dma = pltpu.SemaphoreType.DMA
    tile = (16, 128)
    raw = pl.pallas_call(
        kernel,
        out_shape=jax.ShapeDtypeStruct((STEPS, LAGS, SHARE // 2, CAP), F32),
        in_specs=[pl.BlockSpec(memory_space=pltpu.HBM)] * 3,
        out_specs=pl.BlockSpec(memory_space=pltpu.HBM),
        scratch_shapes=[
            pltpu.SMEM(order.shape, jnp.int32),
            pltpu.SMEM(counts.shape, jnp.int32),
            pltpu.VMEM((NX, 16, SEG), F32),
            pltpu.VMEM((16, K), F32),
            pltpu.VMEM((NX, NX, TILES + 1) + tile, BF16),
            pltpu.VMEM((CLASSES * PLANE, PER) + tile, BF16),
            pltpu.VMEM((CLASSES, PER) + tile, BF16),
            pltpu.VMEM((CLASSES, PER) + tile, BF16),
            pltpu.VMEM((CLASSES, PER) + tile, BF16),
            pltpu.VMEM((STEPS, PLANE, CLASSES, PER) + tile, BF16),
            pltpu.VMEM((2, COLS, 2 * K), BF16),
            pltpu.VMEM((STEPS, 2 * ROWS, COLS), F32),
            pltpu.VMEM((STEPS, ROWS, COLS), BF16),
            pltpu.VMEM((STEPS, ROWS, COLS), BF16),
            pltpu.VMEM((STEPS, LAGS, SHARE // 2, CAP), F32),
            dma((NX + 2,)), dma((CLASSES * NX,)), dma((CLASSES * PLANE,)), dma((NX,)), dma((NX,)),
            dma((STEPS, CLASSES)), dma((STEPS, CLASSES)), dma((STEPS * PLANE, CLASSES)),
            dma((STEPS, 7)), dma((STEPS, PLANE)), dma((STEPS, PLANE)), dma((STEPS,)), dma((STEPS,)), dma((STEPS,)),
            pltpu.SemaphoreType.REGULAR,
        ],
        compiler_params=pltpu.CompilerParams(
            collective_id=0, has_side_effects=True, vmem_limit_bytes=63 << 20),
        cost_estimate=pl.CostEstimate(flops=2 * STEPS * ROWS * COLS * K * DAYS, bytes_accessed=1 << 20, transcendentals=0),
        name="correlate",
    )(order, counts, traces)
    return raw.transpose(0, 2, 1, 3)


def solution(mesh):
    return jax.shard_map(
        per_device, mesh=mesh, in_specs=(P("day", "block", None), P(), P()),
        out_specs=P(None, "day", None, "block"), check_vma=False)
```

```python
import jax
import jax.numpy as jnp
from jax import lax
from jax.experimental import pallas as pl
from jax.experimental.pallas import tpu as pltpu
from jax.sharding import PartitionSpec as P

MESH = pl.DeviceIdType.MESH

SEG = 2400
LAGS = 61
STEPS = 3
HALF = 30
CAP = 64
CLIP = 2.5
DAYS = 8
NZ = 16
NX = 4
PLANE = 4
TILES = 19
K = TILES * 128
SHARE = 16
OWN_SHIFTS = 4
OWNER_SHIFTS = 16
ROWS = OWNER_SHIFTS * SHARE // 2
COLS = OWN_SHIFTS * CAP
CLASSES = 4
PER = 5
F32 = jnp.float32
BF16 = jnp.bfloat16


def kernel(order_hbm, counts_hbm, x_hbm, out_hbm, order, counts, x_ref, wide, gathered, first, far, full,
           shifted, acc, outgoing, incoming, result, load, first_s, first_r, own_s, own_r, far_s, far_r, full_r,
           line_s, core_s, core_r, sum_s, sum_r, out_s, token):
    b = lax.axis_index("block")
    d = lax.axis_index("day")
    z = b // PLANE
    p = b % PLANE
    x = d // 2
    yh = d % 2
    mine = z % CLASSES
    two = 2 - 4 * (p % 2)
    two_x = 2 - 4 * (x % 2)
    q = (p + 2) % PLANE
    mate = p + 1 - 2 * (p % 2)

    def at_device(hop, plane, day):
        return lax.rem(z + hop + NZ, NZ) * PLANE + plane, day

    def day_at(k):
        return lax.rem(x + k, NX) * 2 + yh

    def each(low, high, step):
        def body(n, _):
            step(n)
            return 0
        lax.fori_loop(low, high, body, 0)

    def load_rows(n):
        g = lax.rem(x + 1 + n, NX)
        return pltpu.make_async_copy(
            x_hbm.at[0, pl.ds(pl.multiple_of(g * 16, 16), 16)], x_ref.at[g], load.at[n])

    loads = [pltpu.make_async_copy(order_hbm, order, load.at[NX]),
             pltpu.make_async_copy(counts_hbm, counts, load.at[NX + 1])]

    barrier = pltpu.get_barrier_semaphore()

    def greet(device):
        pl.semaphore_signal(barrier, 1, device_id=device, device_id_type=MESH)

    spots = ((two, q), (two, p), (1, q), (-1, q), (1, p), (-1, p), (0, q))
    for j in (1, 3):
        greet(at_device(CLASSES * j, p, d))
    each(0, NX, lambda n: load_rows(n).start())
    for copy in loads:
        copy.start()

    def greet_sources(plane):
        for hop in (-two, -1, 1):
            greet(at_device(hop, plane, p * 2 + yh))

        @pl.when(jnp.logical_or(plane != p, p != x))
        def _():
            greet(at_device(0, plane, p * 2 + yh))

    each(0, PLANE, greet_sources)
    for hop, plane in spots:
        greet(at_device(-hop, plane, d))
    each(1, NX, lambda k: greet(at_device(0, p, day_at(k))))
    greet(at_device(0, mate, d))
    greet(at_device(0, p, x * 2 + 1 - yh))
    for copy in loads:
        copy.wait()

    hops = (0, 1, -1, two_x)

    def first_copy(i, k):
        to_class = lax.rem(z + hops[i] + NZ, CLASSES)
        return pltpu.make_async_remote_copy(
            gathered.at[x, lax.rem(x + k, NX), pl.ds(to_class * PER, PER)], first.at[i * PLANE + p],
            first_s.at[i * NX + k], first_r.at[i * PLANE + p],
            device_id=at_device(hops[i], x, day_at(k)), device_id_type=MESH)

    def whiten(n):
        g = lax.rem(x + 1 + n, NX)
        load_rows(n).wait()
        rows = x_ref[g]
        centered = rows - jnp.sum(rows, axis=1, keepdims=True) * (1.0 / SEG)
        rms = jnp.sqrt(jnp.sum(centered * centered, axis=1, keepdims=True) * (1.0 / SEG) + 1e-05)
        live = (16 * g + lax.broadcasted_iota(jnp.int32, (16, 1), 0) < counts[b]).astype(F32)
        wide[:, K - 128:] = jnp.zeros((16, 128), F32)
        wide[:, :SEG] = jnp.clip(centered * (1.0 / rms), -CLIP, CLIP) * live
        for i in range(TILES):
            gathered[x, g, i] = wide[:, 128 * i:128 * i + 128].astype(BF16)
        gathered[x, g, TILES] = jnp.zeros((16, 128), BF16)

    each(0, NX, whiten)
    pl.semaphore_wait(barrier, 30 - (p == x).astype(jnp.int32))
    pl.semaphore_signal(token, 1, device_id=at_device(-CLASSES, p, d), device_id_type=MESH)

    def send_first(n):
        k = lax.rem(n + 2, NX)
        for i in (3, 1, 2):
            first_copy(i, k).start()

        @pl.when(jnp.logical_or(k != 0, p != x))
        def _():
            first_copy(0, k).start()

    each(0, NX, send_first)

    @pl.when(p == x)
    def _():
        first[p] = gathered[x, x, pl.ds(mine * PER, PER)]

    def own_copy(k):
        return pltpu.make_async_remote_copy(
            gathered.at[x], gathered.at[x], own_s.at[k], own_r.at[x],
            device_id=at_device(0, p, day_at(k)), device_id_type=MESH)

    each(1, NX, lambda k: own_copy(k).start())

    def shifts_of_day(day):
        def group(g, _):
            rows = jnp.concatenate([gathered[day, g, i] for i in range(TILES)], axis=1)
            for r in range(OWN_SHIFTS):
                rolled = rows if r == 0 else pltpu.roll(rows, r, 1)
                at = pl.multiple_of(r * CAP + g * 16, 16)
                shifted[day % 2, pl.ds(at, 16), pl.ds(pl.multiple_of(day // 2 * K, 128), K)] = rolled
            return 0
        lax.fori_loop(0, CAP // 16, group, 0)

    def own_shifts(k):
        day = lax.rem(x + NX - k, NX)
        pltpu.make_async_remote_copy(
            gathered.at[day], gathered.at[day], own_s.at[k], own_r.at[day],
            device_id=(b, d), device_id_type=MESH).wait_recv()
        shifts_of_day(day)

    shifts_of_day(x)

    def wait_first(j):
        @pl.when(jnp.logical_or(p != x, p != j))
        def _():
            pltpu.make_async_remote_copy(
                first.at[j], first.at[j], first_s.at[0], first_r.at[j],
                device_id=(b, d), device_id_type=MESH).wait_recv()

    each(0, CLASSES * PLANE, wait_first)

    def far_copy(s, j):
        return pltpu.make_async_remote_copy(
            far.at[s, z // CLASSES], far.at[s, z // CLASSES], far_s.at[s, j], far_r.at[s, z // CLASSES],
            device_id=at_device(CLASSES * j, p, d), device_id_type=MESH)

    pl.semaphore_wait(token, 1)
    def send_far(s):
        gap = (z - order[s] // PLANE + NZ) % NZ
        came = jnp.where(gap == 1, 1, jnp.where(gap == NZ - 1, 2, jnp.where(gap == (two + NZ) % NZ, 3, 0)))
        far[s, z // CLASSES] = first[came * PLANE + order[s] % PLANE]
        for j in (2, 1, 3):
            far_copy(s, j).start()

    each(0, STEPS, send_far)

    def piece(s, part, cls, sem, to):
        return pltpu.make_async_remote_copy(
            full.at[s, part, cls], full.at[s, part, cls], sem, full_r.at[s * PLANE + part, cls],
            device_id=to, device_id_type=MESH)

    core = at_device(0, mate, d)

    def spread(s, j):
        hop, plane = spots[j]
        return piece(s, p, mine, line_s.at[s, j], at_device(hop, plane, d))

    def arrival(s, part, cls):
        piece(s, part, cls, line_s.at[0, 0], (b, d)).wait_recv()

    def core_copy(s, part):
        return pltpu.make_async_remote_copy(
            full.at[s, part], full.at[s, part], core_s.at[s, part], core_r.at[s, part],
            device_id=core, device_id_type=MESH)

    others = [lax.rem(z + k, CLASSES) for k in (1, 3, 2)]

    def open_owner(s):
        for j in (1, 3, 2):
            src = lax.rem(z // CLASSES + j, CLASSES)
            pltpu.make_async_remote_copy(
                far.at[s, src], far.at[s, src], far_s.at[s, j], far_r.at[s, src],
                device_id=(b, d), device_id_type=MESH).wait_recv()
        owner_z = order[s] // PLANE
        gap = (mine - owner_z + NZ) % CLASSES
        step = jnp.where(gap == 3, -1, jnp.where(gap == 2, two, gap))
        sender = (owner_z + step + NZ) % NZ
        best = far[s, 0]
        for n in range(1, CLASSES):
            best = jnp.where(sender // CLASSES == n, far[s, n], best)
        full[s, p, mine] = best
        for j in range(len(spots)):
            spread(s, j).start()

    def pass_on(s):
        for cls in others:
            arrival(s, p, cls)
        core_copy(s, p).start()
        arrival(s, q, mine)
        for cls in others:
            arrival(s, q, cls)
        core_copy(s, q).start()

    def from_core(s):
        for part in (mate, (mate + 2) % PLANE):
            core_copy(s, part).wait_recv()

    def add_days(s, odd):
        left = []
        for k in range(2):
            rows = jnp.concatenate(
                [full[s, odd + 2 * k, t // PER, t % PER] for t in range(TILES)], axis=1)
            left.append(jnp.concatenate(
                [pltpu.roll(rows, (HALF - OWN_SHIFTS * n) % K, 1) for n in range(OWNER_SHIFTS)], axis=0))
        return lax.dot_general(jnp.concatenate(left, axis=1), shifted[odd], (((1,), (1,)), ((), ())),
                               preferred_element_type=F32)

    def sum_copy(s):
        return pltpu.make_async_remote_copy(
            outgoing.at[s], incoming.at[s], sum_s.at[s], sum_r.at[s],
            device_id=at_device(0, p, x * 2 + 1 - yh), device_id_type=MESH)

    def out_copy(s):
        return pltpu.make_async_copy(result.at[s], out_hbm.at[s], out_s.at[s])

    def halves(s):
        whole = acc[s].reshape(OWNER_SHIFTS, 2, SHARE // 2, COLS)
        return whole[:, 0].reshape(ROWS, COLS), whole[:, 1].reshape(ROWS, COLS)

    def to_partner(s):
        top, low = halves(s)
        outgoing[s] = jnp.where(yh == 0, low, top).astype(BF16)
        sum_copy(s).start()

    def finish(s):
        sum_copy(s).wait_recv()
        top, low = halves(s)
        sums = (jnp.where(yh == 0, top, low) + incoming[s].astype(F32)) * (float(DAYS * SEG) ** -0.5)
        for lag in range(LAGS):
            n, r = lag // OWN_SHIFTS, lag % OWN_SHIFTS
            result[s, lag] = sums[8 * n:8 * n + 8, CAP * r:CAP * r + CAP]
        out_copy(s).start()

    each(0, STEPS, open_owner)
    each(1, NX, own_shifts)
    pass_on(0)

    def owner(s):
        def part(h):
            @pl.when(h == 1)
            def _():
                @pl.when(s < STEPS - 1)
                def _():
                    pass_on(s + 1)
                from_core(s)
            sums = add_days(s, lax.rem(p + h, 2))

            @pl.when(h == 0)
            def _():
                acc[s] = sums

            @pl.when(h == 1)
            def _():
                acc[s] += sums
        each(0, 2, part)
        to_partner(s)

    each(0, STEPS, owner)

    def sent(k):
        for i in range(1, CLASSES):
            first_copy(i, k).wait_send()

        @pl.when(jnp.logical_or(k != 0, p != x))
        def _():
            first_copy(0, k).wait_send()

        @pl.when(k > 0)
        def _():
            own_copy(k).wait_send()

    def owner_sent(s):
        for k in range(1, NX):
            far_copy(s, k).wait_send()
        for j in range(len(spots)):
            spread(s, j).wait_send()
        for part in (p, q):
            core_copy(s, part).wait_send()

    each(0, NX, sent)
    each(0, STEPS, owner_sent)
    each(0, STEPS, finish)

    def done(s):
        sum_copy(s).wait_send()
        out_copy(s).wait()

    each(0, STEPS, done)


def per_device(traces, counts, order):
    dma = pltpu.SemaphoreType.DMA
    tile = (16, 128)
    raw = pl.pallas_call(
        kernel,
        out_shape=jax.ShapeDtypeStruct((STEPS, LAGS, SHARE // 2, CAP), F32),
        in_specs=[pl.BlockSpec(memory_space=pltpu.HBM)] * 3,
        out_specs=pl.BlockSpec(memory_space=pltpu.HBM),
        scratch_shapes=[
            pltpu.SMEM(order.shape, jnp.int32),
            pltpu.SMEM(counts.shape, jnp.int32),
            pltpu.VMEM((NX, 16, SEG), F32),
            pltpu.VMEM((16, K), F32),
            pltpu.VMEM((NX, NX, TILES + 1) + tile, BF16),
            pltpu.VMEM((CLASSES * PLANE, PER) + tile, BF16),
            pltpu.VMEM((STEPS, CLASSES, PER) + tile, BF16),
            pltpu.VMEM((STEPS, PLANE, CLASSES, PER) + tile, BF16),
            pltpu.VMEM((2, COLS, 2 * K), BF16),
            pltpu.VMEM((STEPS, 2 * ROWS, COLS), F32),
            pltpu.VMEM((STEPS, ROWS, COLS), BF16),
            pltpu.VMEM((STEPS, ROWS, COLS), BF16),
            pltpu.VMEM((STEPS, LAGS, SHARE // 2, CAP), F32),
            dma((NX + 2,)), dma((CLASSES * NX,)), dma((CLASSES * PLANE,)), dma((NX,)), dma((NX,)),
            dma((STEPS, CLASSES)), dma((STEPS, CLASSES)), dma((STEPS * PLANE, CLASSES)),
            dma((STEPS, 7)), dma((STEPS, PLANE)), dma((STEPS, PLANE)), dma((STEPS,)), dma((STEPS,)), dma((STEPS,)),
            pltpu.SemaphoreType.REGULAR,
        ],
        compiler_params=pltpu.CompilerParams(
            collective_id=0, has_side_effects=True, vmem_limit_bytes=63 << 20),
        cost_estimate=pl.CostEstimate(flops=2 * STEPS * ROWS * COLS * K * DAYS, bytes_accessed=1 << 20, transcendentals=0),
        name="correlate",
    )(order, counts, traces)
    return raw.transpose(0, 2, 1, 3)


def solution(mesh):
    return jax.shard_map(
        per_device, mesh=mesh, in_specs=(P("day", "block", None), P(), P()),
        out_specs=P(None, "day", None, "block"), check_vma=False)
```

```python
import jax
import jax.numpy as jnp
from jax import lax
from jax.experimental import pallas as pl
from jax.experimental.pallas import tpu as pltpu
from jax.sharding import PartitionSpec as P

MESH = pl.DeviceIdType.MESH

SEG = 2400
LAGS = 61
STEPS = 3
HALF = 30
CAP = 64
CLIP = 2.5
DAYS = 8
NZ = 16
NX = 4
PLANE = 4
TILES = 19
K = TILES * 128
SHARE = 16
OWN_SHIFTS = 4
OWNER_SHIFTS = 16
ROWS = OWNER_SHIFTS * SHARE // 2
COLS = OWN_SHIFTS * CAP
CLASSES = 4
PER = 5
F32 = jnp.float32
BF16 = jnp.bfloat16


def kernel(order_hbm, counts_hbm, x_hbm, out_hbm, order, counts, x_ref, wide, gathered, first, far, full,
           shifted, acc, outgoing, incoming, result, load, first_s, first_r, own_s, own_r, far_s, far_r, full_r,
           line_s, core_s, core_r, sum_s, sum_r, out_s, token):
    b = lax.axis_index("block")
    d = lax.axis_index("day")
    z = b // PLANE
    p = b % PLANE
    x = d // 2
    yh = d % 2
    mine = z % CLASSES
    two = 2 - 4 * (p % 2)
    two_x = 2 - 4 * (x % 2)
    q = (p + 2) % PLANE
    mate = p + 1 - 2 * (p % 2)

    def at_device(hop, plane, day):
        return lax.rem(z + hop + NZ, NZ) * PLANE + plane, day

    def day_at(k):
        return lax.rem(x + k, NX) * 2 + yh

    def each(low, high, step):
        def body(n, _):
            step(n)
            return 0
        lax.fori_loop(low, high, body, 0)

    def load_rows(n):
        g = lax.rem(x + 2 + n, NX)
        return pltpu.make_async_copy(
            x_hbm.at[0, pl.ds(pl.multiple_of(g * 16, 16), 16)], x_ref.at[g], load.at[n])

    loads = [pltpu.make_async_copy(order_hbm, order, load.at[NX]),
             pltpu.make_async_copy(counts_hbm, counts, load.at[NX + 1])]

    barrier = pltpu.get_barrier_semaphore()

    def greet(device):
        pl.semaphore_signal(barrier, 1, device_id=device, device_id_type=MESH)

    spots = ((two, q), (two, p), (1, q), (-1, q), (1, p), (-1, p), (0, q))
    for j in (1, 3):
        greet(at_device(CLASSES * j, p, d))
    each(0, NX, lambda n: load_rows(n).start())
    for copy in loads:
        copy.start()

    def greet_sources(plane):
        for hop in (-two, -1, 1):
            greet(at_device(hop, plane, p * 2 + yh))

        @pl.when(jnp.logical_or(plane != p, p != x))
        def _():
            greet(at_device(0, plane, p * 2 + yh))

    each(0, PLANE, greet_sources)
    for hop, plane in spots:
        greet(at_device(-hop, plane, d))
    each(1, NX, lambda k: greet(at_device(0, p, day_at(k))))
    greet(at_device(0, mate, d))
    greet(at_device(0, p, x * 2 + 1 - yh))
    for copy in loads:
        copy.wait()

    hops = (0, 1, -1, two_x)

    def first_copy(i, k):
        to_class = lax.rem(z + hops[i] + NZ, CLASSES)
        return pltpu.make_async_remote_copy(
            gathered.at[x, lax.rem(x + k, NX), pl.ds(to_class * PER, PER)], first.at[i * PLANE + p],
            first_s.at[i * NX + k], first_r.at[i * PLANE + p],
            device_id=at_device(hops[i], x, day_at(k)), device_id_type=MESH)

    def whiten(n):
        g = lax.rem(x + 2 + n, NX)
        load_rows(n).wait()
        rows = x_ref[g]
        centered = rows - jnp.sum(rows, axis=1, keepdims=True) * (1.0 / SEG)
        rms = jnp.sqrt(jnp.sum(centered * centered, axis=1, keepdims=True) * (1.0 / SEG) + 1e-05)
        live = (16 * g + lax.broadcasted_iota(jnp.int32, (16, 1), 0) < counts[b]).astype(F32)
        wide[:, K - 128:] = jnp.zeros((16, 128), F32)
        wide[:, :SEG] = jnp.clip(centered * (1.0 / rms), -CLIP, CLIP) * live
        for i in range(TILES):
            gathered[x, g, i] = wide[:, 128 * i:128 * i + 128].astype(BF16)
        gathered[x, g, TILES] = jnp.zeros((16, 128), BF16)

    def send_first(n):
        whiten(n)

        @pl.when(n == 0)
        def _():
            pl.semaphore_wait(barrier, 30 - (p == x).astype(jnp.int32))
            pl.semaphore_signal(token, 1, device_id=at_device(-CLASSES, p, d), device_id_type=MESH)

        k = lax.rem(n + 2, NX)
        for i in (3, 1, 2):
            first_copy(i, k).start()

        @pl.when(jnp.logical_or(k != 0, p != x))
        def _():
            first_copy(0, k).start()

    each(0, NX, send_first)

    @pl.when(p == x)
    def _():
        first[p] = gathered[x, x, pl.ds(mine * PER, PER)]

    def own_copy(k):
        return pltpu.make_async_remote_copy(
            gathered.at[x], gathered.at[x], own_s.at[k], own_r.at[x],
            device_id=at_device(0, p, day_at(k)), device_id_type=MESH)

    each(1, NX, lambda k: own_copy(k).start())

    def shifts_of_day(day):
        def group(g, _):
            rows = jnp.concatenate([gathered[day, g, i] for i in range(TILES)], axis=1)
            for r in range(OWN_SHIFTS):
                rolled = rows if r == 0 else pltpu.roll(rows, r, 1)
                at = pl.multiple_of(r * CAP + g * 16, 16)
                shifted[day % 2, pl.ds(at, 16), pl.ds(pl.multiple_of(day // 2 * K, 128), K)] = rolled
            return 0
        lax.fori_loop(0, CAP // 16, group, 0)

    def own_shifts(k):
        day = lax.rem(x + NX - k, NX)
        pltpu.make_async_remote_copy(
            gathered.at[day], gathered.at[day], own_s.at[k], own_r.at[day],
            device_id=(b, d), device_id_type=MESH).wait_recv()
        shifts_of_day(day)

    shifts_of_day(x)

    def wait_first(j):
        @pl.when(jnp.logical_or(p != x, p != j))
        def _():
            pltpu.make_async_remote_copy(
                first.at[j], first.at[j], first_s.at[0], first_r.at[j],
                device_id=(b, d), device_id_type=MESH).wait_recv()

    each(0, CLASSES * PLANE, wait_first)

    def far_copy(s, j):
        return pltpu.make_async_remote_copy(
            far.at[s, z // CLASSES], far.at[s, z // CLASSES], far_s.at[s, j], far_r.at[s, z // CLASSES],
            device_id=at_device(CLASSES * j, p, d), device_id_type=MESH)

    pl.semaphore_wait(token, 1)
    def send_far(s):
        gap = (z - order[s] // PLANE + NZ) % NZ
        came = jnp.where(gap == 1, 1, jnp.where(gap == NZ - 1, 2, jnp.where(gap == (two + NZ) % NZ, 3, 0)))
        far[s, z // CLASSES] = first[came * PLANE + order[s] % PLANE]
        for j in (2, 1, 3):
            far_copy(s, j).start()

    each(0, STEPS, send_far)

    def piece(s, part, cls, sem, to):
        return pltpu.make_async_remote_copy(
            full.at[s, part, cls], full.at[s, part, cls], sem, full_r.at[s * PLANE + part, cls],
            device_id=to, device_id_type=MESH)

    core = at_device(0, mate, d)

    def spread(s, j):
        hop, plane = spots[j]
        return piece(s, p, mine, line_s.at[s, j], at_device(hop, plane, d))

    def arrival(s, part, cls):
        piece(s, part, cls, line_s.at[0, 0], (b, d)).wait_recv()

    def core_copy(s, part):
        return pltpu.make_async_remote_copy(
            full.at[s, part], full.at[s, part], core_s.at[s, part], core_r.at[s, part],
            device_id=core, device_id_type=MESH)

    others = [lax.rem(z + k, CLASSES) for k in (1, 3, 2)]

    def open_owner(s):
        for j in (1, 3, 2):
            src = lax.rem(z // CLASSES + j, CLASSES)
            pltpu.make_async_remote_copy(
                far.at[s, src], far.at[s, src], far_s.at[s, j], far_r.at[s, src],
                device_id=(b, d), device_id_type=MESH).wait_recv()
        owner_z = order[s] // PLANE
        gap = (mine - owner_z + NZ) % CLASSES
        step = jnp.where(gap == 3, -1, jnp.where(gap == 2, two, gap))
        sender = (owner_z + step + NZ) % NZ
        best = far[s, 0]
        for n in range(1, CLASSES):
            best = jnp.where(sender // CLASSES == n, far[s, n], best)
        full[s, p, mine] = best
        for j in range(len(spots)):
            spread(s, j).start()

    def pass_on(s):
        for cls in others:
            arrival(s, p, cls)
        core_copy(s, p).start()
        arrival(s, q, mine)
        for cls in others:
            arrival(s, q, cls)
        core_copy(s, q).start()

    def from_core(s):
        for part in (mate, (mate + 2) % PLANE):
            core_copy(s, part).wait_recv()

    def add_days(s, odd):
        left = []
        for k in range(2):
            rows = jnp.concatenate(
                [full[s, odd + 2 * k, t // PER, t % PER] for t in range(TILES)], axis=1)
            left.append(jnp.concatenate(
                [pltpu.roll(rows, (HALF - OWN_SHIFTS * n) % K, 1) for n in range(OWNER_SHIFTS)], axis=0))
        return lax.dot_general(jnp.concatenate(left, axis=1), shifted[odd], (((1,), (1,)), ((), ())),
                               preferred_element_type=F32)

    def sum_copy(s):
        return pltpu.make_async_remote_copy(
            outgoing.at[s], incoming.at[s], sum_s.at[s], sum_r.at[s],
            device_id=at_device(0, p, x * 2 + 1 - yh), device_id_type=MESH)

    def out_copy(s):
        return pltpu.make_async_copy(result.at[s], out_hbm.at[s], out_s.at[s])

    def halves(s):
        whole = acc[s].reshape(OWNER_SHIFTS, 2, SHARE // 2, COLS)
        return whole[:, 0].reshape(ROWS, COLS), whole[:, 1].reshape(ROWS, COLS)

    def to_partner(s):
        top, low = halves(s)
        outgoing[s] = jnp.where(yh == 0, low, top).astype(BF16)
        sum_copy(s).start()

    def finish(s):
        sum_copy(s).wait_recv()
        top, low = halves(s)
        sums = jnp.where(yh == 0, top, low) + incoming[s].astype(F32)
        for lag in range(LAGS):
            n, r = lag // OWN_SHIFTS, lag % OWN_SHIFTS
            result[s, lag] = sums[8 * n:8 * n + 8, CAP * r:CAP * r + CAP]
        out_copy(s).start()

    each(0, STEPS, open_owner)
    each(1, NX, own_shifts)
    pass_on(0)

    def owner(s):
        def part(h):
            @pl.when(h == 1)
            def _():
                @pl.when(s < STEPS - 1)
                def _():
                    pass_on(s + 1)
                from_core(s)
            sums = add_days(s, lax.rem(p + h, 2))

            @pl.when(h == 0)
            def _():
                acc[s] = sums

            @pl.when(h == 1)
            def _():
                acc[s] += sums
        each(0, 2, part)
        to_partner(s)

    each(0, STEPS, owner)

    def sent(k):
        for i in range(1, CLASSES):
            first_copy(i, k).wait_send()

        @pl.when(jnp.logical_or(k != 0, p != x))
        def _():
            first_copy(0, k).wait_send()

        @pl.when(k > 0)
        def _():
            own_copy(k).wait_send()

    def owner_sent(s):
        for k in range(1, NX):
            far_copy(s, k).wait_send()
        for j in range(len(spots)):
            spread(s, j).wait_send()
        for part in (p, q):
            core_copy(s, part).wait_send()

    each(0, NX, sent)
    each(0, STEPS, owner_sent)
    each(0, STEPS, finish)

    def done(s):
        sum_copy(s).wait_send()
        out_copy(s).wait()

    each(0, STEPS, done)


def per_device(traces, counts, order):
    dma = pltpu.SemaphoreType.DMA
    tile = (16, 128)
    raw = pl.pallas_call(
        kernel,
        out_shape=jax.ShapeDtypeStruct((STEPS, LAGS, SHARE // 2, CAP), F32),
        in_specs=[pl.BlockSpec(memory_space=pltpu.HBM)] * 3,
        out_specs=pl.BlockSpec(memory_space=pltpu.HBM),
        scratch_shapes=[
            pltpu.SMEM(order.shape, jnp.int32),
            pltpu.SMEM(counts.shape, jnp.int32),
            pltpu.VMEM((NX, 16, SEG), F32),
            pltpu.VMEM((16, K), F32),
            pltpu.VMEM((NX, NX, TILES + 1) + tile, BF16),
            pltpu.VMEM((CLASSES * PLANE, PER) + tile, BF16),
            pltpu.VMEM((STEPS, CLASSES, PER) + tile, BF16),
            pltpu.VMEM((STEPS, PLANE, CLASSES, PER) + tile, BF16),
            pltpu.VMEM((2, COLS, 2 * K), BF16),
            pltpu.VMEM((STEPS, 2 * ROWS, COLS), F32),
            pltpu.VMEM((STEPS, ROWS, COLS), BF16),
            pltpu.VMEM((STEPS, ROWS, COLS), BF16),
            pltpu.VMEM((STEPS, LAGS, SHARE // 2, CAP), F32),
            dma((NX + 2,)), dma((CLASSES * NX,)), dma((CLASSES * PLANE,)), dma((NX,)), dma((NX,)),
            dma((STEPS, CLASSES)), dma((STEPS, CLASSES)), dma((STEPS * PLANE, CLASSES)),
            dma((STEPS, 7)), dma((STEPS, PLANE)), dma((STEPS, PLANE)), dma((STEPS,)), dma((STEPS,)), dma((STEPS,)),
            pltpu.SemaphoreType.REGULAR,
        ],
        compiler_params=pltpu.CompilerParams(
            collective_id=0, has_side_effects=True, vmem_limit_bytes=63 << 20),
        cost_estimate=pl.CostEstimate(flops=2 * STEPS * ROWS * COLS * K * DAYS, bytes_accessed=1 << 20, transcendentals=0),
        name="correlate",
    )(order, counts, traces)
    return raw.transpose(0, 2, 1, 3) * (float(DAYS * SEG) ** -0.5)


def solution(mesh):
    return jax.shard_map(
        per_device, mesh=mesh, in_specs=(P("day", "block", None), P(), P()),
        out_specs=P(None, "day", None, "block"), check_vma=False)
```

```python
import jax
import jax.numpy as jnp
from jax import lax
from jax.experimental import pallas as pl
from jax.experimental.pallas import tpu as pltpu
from jax.sharding import PartitionSpec as P

MESH = pl.DeviceIdType.MESH

SEG = 2400
LAGS = 61
STEPS = 3
HALF = 30
CAP = 64
CLIP = 2.5
DAYS = 8
N_BLOCK = 64
NZ = 16
NX = 4
PLANE = 4
TILES = 19
K = TILES * 128
SHARE = 16
OWN_SHIFTS = 4
OWNER_SHIFTS = 16
ROWS = OWNER_SHIFTS * SHARE // 2
COLS = OWN_SHIFTS * CAP
CLASSES = 4
PER = 5
F32 = jnp.float32
BF16 = jnp.bfloat16


def kernel(table_hbm, x_hbm, out_hbm, table, x_ref, wide, gathered, first, far, full,
           shifted, acc, outgoing, incoming, result, load, first_s, first_r, own_s, own_r, far_s, far_r, full_r,
           line_s, core_s, core_r, sum_s, sum_r, out_s, token):
    b = lax.axis_index("block")
    d = lax.axis_index("day")
    z = b // PLANE
    p = b % PLANE
    x = d // 2
    yh = d % 2
    mine = z % CLASSES
    two = 2 - 4 * (p % 2)
    two_x = 2 - 4 * (x % 2)
    q = (p + 2) % PLANE
    mate = p + 1 - 2 * (p % 2)

    def at_device(hop, plane, day):
        return lax.rem(z + hop + NZ, NZ) * PLANE + plane, day

    def day_at(k):
        return lax.rem(x + k, NX) * 2 + yh

    def each(low, high, step):
        def body(n, _):
            step(n)
            return 0
        lax.fori_loop(low, high, body, 0)

    def load_rows(n):
        g = lax.rem(x + 1 + n, NX)
        return pltpu.make_async_copy(
            x_hbm.at[0, pl.ds(pl.multiple_of(g * 16, 16), 16)], x_ref.at[g], load.at[n])

    load_table = pltpu.make_async_copy(table_hbm, table, load.at[NX])

    barrier = pltpu.get_barrier_semaphore()

    def greet(device):
        pl.semaphore_signal(barrier, 1, device_id=device, device_id_type=MESH)

    spots = ((two, q), (two, p), (1, q), (-1, q), (1, p), (-1, p), (0, q))
    for j in (1, 3):
        greet(at_device(CLASSES * j, p, d))
    each(0, NX, lambda n: load_rows(n).start())
    load_table.start()

    def greet_sources(plane):
        for hop in (-two, -1, 1):
            greet(at_device(hop, plane, p * 2 + yh))

        @pl.when(jnp.logical_or(plane != p, p != x))
        def _():
            greet(at_device(0, plane, p * 2 + yh))

    each(0, PLANE, greet_sources)
    for hop, plane in spots:
        greet(at_device(-hop, plane, d))
    each(1, NX, lambda k: greet(at_device(0, p, day_at(k))))
    greet(at_device(0, mate, d))
    greet(at_device(0, p, x * 2 + 1 - yh))
    load_table.wait()

    hops = (0, 1, -1, two_x)

    def first_copy(i, k):
        to_class = lax.rem(z + hops[i] + NZ, CLASSES)
        return pltpu.make_async_remote_copy(
            gathered.at[x, lax.rem(x + k, NX), pl.ds(to_class * PER, PER)], first.at[i * PLANE + p],
            first_s.at[i * NX + k], first_r.at[i * PLANE + p],
            device_id=at_device(hops[i], x, day_at(k)), device_id_type=MESH)

    def whiten(n):
        g = lax.rem(x + 1 + n, NX)
        load_rows(n).wait()
        rows = x_ref[g]
        centered = rows - jnp.sum(rows, axis=1, keepdims=True) * (1.0 / SEG)
        rms = jnp.sqrt(jnp.sum(centered * centered, axis=1, keepdims=True) * (1.0 / SEG) + 1e-05)
        live = (16 * g + lax.broadcasted_iota(jnp.int32, (16, 1), 0) < table[b]).astype(F32)
        wide[:, K - 128:] = jnp.zeros((16, 128), F32)
        wide[:, :SEG] = jnp.clip(centered * (1.0 / rms), -CLIP, CLIP) * live
        for i in range(TILES):
            gathered[x, g, i] = wide[:, 128 * i:128 * i + 128].astype(BF16)
        gathered[x, g, TILES] = jnp.zeros((16, 128), BF16)

    each(0, NX, whiten)
    pl.semaphore_wait(barrier, 30 - (p == x).astype(jnp.int32))
    pl.semaphore_signal(token, 1, device_id=at_device(-CLASSES, p, d), device_id_type=MESH)

    def send_first(n):
        k = lax.rem(n + 2, NX)
        for i in (3, 1, 2):
            first_copy(i, k).start()

        @pl.when(jnp.logical_or(k != 0, p != x))
        def _():
            first_copy(0, k).start()

    each(0, NX, send_first)

    @pl.when(p == x)
    def _():
        first[p] = gathered[x, x, pl.ds(mine * PER, PER)]

    def own_copy(k):
        return pltpu.make_async_remote_copy(
            gathered.at[x], gathered.at[x], own_s.at[k], own_r.at[x],
            device_id=at_device(0, p, day_at(k)), device_id_type=MESH)

    each(1, NX, lambda k: own_copy(k).start())

    def shifts_of_day(day):
        def group(g, _):
            rows = jnp.concatenate([gathered[day, g, i] for i in range(TILES)], axis=1)
            for r in range(OWN_SHIFTS):
                rolled = rows if r == 0 else pltpu.roll(rows, r, 1)
                at = pl.multiple_of(r * CAP + g * 16, 16)
                shifted[day % 2, pl.ds(at, 16), pl.ds(pl.multiple_of(day // 2 * K, 128), K)] = rolled
            return 0
        lax.fori_loop(0, CAP // 16, group, 0)

    def own_shifts(k):
        day = lax.rem(x + NX - k, NX)
        pltpu.make_async_remote_copy(
            gathered.at[day], gathered.at[day], own_s.at[k], own_r.at[day],
            device_id=(b, d), device_id_type=MESH).wait_recv()
        shifts_of_day(day)

    shifts_of_day(x)

    def wait_first(j):
        @pl.when(jnp.logical_or(p != x, p != j))
        def _():
            pltpu.make_async_remote_copy(
                first.at[j], first.at[j], first_s.at[0], first_r.at[j],
                device_id=(b, d), device_id_type=MESH).wait_recv()

    each(0, CLASSES * PLANE, wait_first)

    def far_copy(s, j):
        return pltpu.make_async_remote_copy(
            far.at[s, z // CLASSES], far.at[s, z // CLASSES], far_s.at[s, j], far_r.at[s, z // CLASSES],
            device_id=at_device(CLASSES * j, p, d), device_id_type=MESH)

    pl.semaphore_wait(token, 1)
    def send_far(s):
        gap = (z - table[N_BLOCK + s] // PLANE + NZ) % NZ
        came = jnp.where(gap == 1, 1, jnp.where(gap == NZ - 1, 2, jnp.where(gap == (two + NZ) % NZ, 3, 0)))
        far[s, z // CLASSES] = first[came * PLANE + table[N_BLOCK + s] % PLANE]
        for j in (2, 1, 3):
            far_copy(s, j).start()

    each(0, STEPS, send_far)

    def piece(s, part, cls, sem, to):
        return pltpu.make_async_remote_copy(
            full.at[s, part, cls], full.at[s, part, cls], sem, full_r.at[s * PLANE + part, cls],
            device_id=to, device_id_type=MESH)

    core = at_device(0, mate, d)

    def spread(s, j):
        hop, plane = spots[j]
        return piece(s, p, mine, line_s.at[s, j], at_device(hop, plane, d))

    def arrival(s, part, cls):
        piece(s, part, cls, line_s.at[0, 0], (b, d)).wait_recv()

    def core_copy(s, part):
        return pltpu.make_async_remote_copy(
            full.at[s, part], full.at[s, part], core_s.at[s, part], core_r.at[s, part],
            device_id=core, device_id_type=MESH)

    others = [lax.rem(z + k, CLASSES) for k in (1, 3, 2)]

    def open_owner(s):
        for j in (1, 3, 2):
            src = lax.rem(z // CLASSES + j, CLASSES)
            pltpu.make_async_remote_copy(
                far.at[s, src], far.at[s, src], far_s.at[s, j], far_r.at[s, src],
                device_id=(b, d), device_id_type=MESH).wait_recv()
        owner_z = table[N_BLOCK + s] // PLANE
        gap = (mine - owner_z + NZ) % CLASSES
        step = jnp.where(gap == 3, -1, jnp.where(gap == 2, two, gap))
        sender = (owner_z + step + NZ) % NZ
        best = far[s, 0]
        for n in range(1, CLASSES):
            best = jnp.where(sender // CLASSES == n, far[s, n], best)
        full[s, p, mine] = best
        for j in range(len(spots)):
            spread(s, j).start()

    def pass_on(s):
        for cls in others:
            arrival(s, p, cls)
        core_copy(s, p).start()
        arrival(s, q, mine)
        for cls in others:
            arrival(s, q, cls)
        core_copy(s, q).start()

    def from_core(s):
        for part in (mate, (mate + 2) % PLANE):
            core_copy(s, part).wait_recv()

    def add_days(s, odd):
        left = []
        for k in range(2):
            rows = jnp.concatenate(
                [full[s, odd + 2 * k, t // PER, t % PER] for t in range(TILES)], axis=1)
            left.append(jnp.concatenate(
                [pltpu.roll(rows, (HALF - OWN_SHIFTS * n) % K, 1) for n in range(OWNER_SHIFTS)], axis=0))
        return lax.dot_general(jnp.concatenate(left, axis=1), shifted[odd], (((1,), (1,)), ((), ())),
                               preferred_element_type=F32)

    def sum_copy(s):
        return pltpu.make_async_remote_copy(
            outgoing.at[s], incoming.at[s], sum_s.at[s], sum_r.at[s],
            device_id=at_device(0, p, x * 2 + 1 - yh), device_id_type=MESH)

    def out_copy(s):
        return pltpu.make_async_copy(result.at[s, pl.ds(0, LAGS)], out_hbm.at[s], out_s.at[s])

    def half_rows(s, n, half):
        return acc[s, pl.ds(pl.multiple_of(16 * n + 8 * half, 8), 8), :]

    def to_partner(s):
        def pair(n):
            rows = jnp.concatenate([half_rows(s, 2 * n, 1 - yh), half_rows(s, 2 * n + 1, 1 - yh)], axis=0)
            outgoing[s, pl.ds(pl.multiple_of(16 * n, 16), 16), :] = rows.astype(BF16)
        each(0, OWNER_SHIFTS // 2, pair)
        sum_copy(s).start()

    def finish(s):
        sum_copy(s).wait_recv()

        def pair(n):
            got = incoming[s, pl.ds(pl.multiple_of(16 * n, 16), 16), :].astype(F32)
            for k in range(2):
                sums = (half_rows(s, 2 * n + k, yh) + got[8 * k:8 * k + 8]) * (float(DAYS * SEG) ** -0.5)
                for r in range(OWN_SHIFTS):
                    result[s, OWN_SHIFTS * (2 * n + k) + r] = sums[:, CAP * r:CAP * r + CAP]
        each(0, OWNER_SHIFTS // 2, pair)
        out_copy(s).start()

    each(0, STEPS, open_owner)
    each(1, NX, own_shifts)
    pass_on(0)

    def owner(s):
        def part(h):
            @pl.when(h == 1)
            def _():
                @pl.when(s < STEPS - 1)
                def _():
                    pass_on(s + 1)
                from_core(s)
            sums = add_days(s, lax.rem(p + h, 2))

            @pl.when(h == 0)
            def _():
                acc[s] = sums

            @pl.when(h == 1)
            def _():
                acc[s] += sums
        each(0, 2, part)
        to_partner(s)

    each(0, STEPS, owner)

    def sent(k):
        for i in range(1, CLASSES):
            first_copy(i, k).wait_send()

        @pl.when(jnp.logical_or(k != 0, p != x))
        def _():
            first_copy(0, k).wait_send()

        @pl.when(k > 0)
        def _():
            own_copy(k).wait_send()

    def owner_sent(s):
        for k in range(1, NX):
            far_copy(s, k).wait_send()
        for j in range(len(spots)):
            spread(s, j).wait_send()
        for part in (p, q):
            core_copy(s, part).wait_send()

    each(0, NX, sent)
    each(0, STEPS, owner_sent)
    each(0, STEPS, finish)

    def done(s):
        sum_copy(s).wait_send()
        out_copy(s).wait()

    each(0, STEPS, done)


def per_device(traces, counts, order):
    dma = pltpu.SemaphoreType.DMA
    tile = (16, 128)
    raw = pl.pallas_call(
        kernel,
        out_shape=jax.ShapeDtypeStruct((STEPS, LAGS, SHARE // 2, CAP), F32),
        in_specs=[pl.BlockSpec(memory_space=pltpu.HBM)] * 2,
        out_specs=pl.BlockSpec(memory_space=pltpu.HBM),
        scratch_shapes=[
            pltpu.SMEM((2 * N_BLOCK,), jnp.int32),
            pltpu.VMEM((NX, 16, SEG), F32),
            pltpu.VMEM((16, K), F32),
            pltpu.VMEM((NX, NX, TILES + 1) + tile, BF16),
            pltpu.VMEM((CLASSES * PLANE, PER) + tile, BF16),
            pltpu.VMEM((STEPS, CLASSES, PER) + tile, BF16),
            pltpu.VMEM((STEPS, PLANE, CLASSES, PER) + tile, BF16),
            pltpu.VMEM((2, COLS, 2 * K), BF16),
            pltpu.VMEM((STEPS, 2 * ROWS, COLS), F32),
            pltpu.VMEM((STEPS, ROWS, COLS), BF16),
            pltpu.VMEM((STEPS, ROWS, COLS), BF16),
            pltpu.VMEM((STEPS, OWN_SHIFTS * OWNER_SHIFTS, SHARE // 2, CAP), F32),
            dma((NX + 1,)), dma((CLASSES * NX,)), dma((CLASSES * PLANE,)), dma((NX,)), dma((NX,)),
            dma((STEPS, CLASSES)), dma((STEPS, CLASSES)), dma((STEPS * PLANE, CLASSES)),
            dma((STEPS, 7)), dma((STEPS, PLANE)), dma((STEPS, PLANE)), dma((STEPS,)), dma((STEPS,)), dma((STEPS,)),
            pltpu.SemaphoreType.REGULAR,
        ],
        compiler_params=pltpu.CompilerParams(
            collective_id=0, has_side_effects=True, vmem_limit_bytes=48 << 20),
        cost_estimate=pl.CostEstimate(flops=2 * STEPS * ROWS * COLS * K * DAYS, bytes_accessed=1 << 20, transcendentals=0),
        name="correlate",
    )(jnp.concatenate([counts, order]), traces)
    return raw.transpose(0, 2, 1, 3)


def solution(mesh):
    return jax.shard_map(
        per_device, mesh=mesh, in_specs=(P("day", "block", None), P(), P()),
        out_specs=P(None, "day", None, "block"), check_vma=False)
```

```python
import jax
import jax.numpy as jnp
from jax import lax
from jax.experimental import pallas as pl
from jax.experimental.pallas import tpu as pltpu
from jax.sharding import PartitionSpec as P

MESH = pl.DeviceIdType.MESH

SEG = 2400
LAGS = 61
STEPS = 3
HALF = 30
CAP = 64
CLIP = 2.5
DAYS = 8
N_BLOCK = 64
NZ = 16
NX = 4
PLANE = 4
TILES = 19
K = TILES * 128
SHARE = 16
OWN_SHIFTS = 4
OWNER_SHIFTS = 16
ROWS = OWNER_SHIFTS * SHARE // 2
COLS = OWN_SHIFTS * CAP
CLASSES = 4
PER = 5
F32 = jnp.float32
BF16 = jnp.bfloat16


def kernel(table_hbm, x_hbm, out_ref, table, x_ref, wide, gathered, first, far, full,
           shifted, acc, outgoing, incoming, load, first_s, first_r, own_s, own_r, far_s, far_r, full_r,
           line_s, core_s, core_r, sum_s, sum_r, token):
    b = lax.axis_index("block")
    d = lax.axis_index("day")
    z = b // PLANE
    p = b % PLANE
    x = d // 2
    yh = d % 2
    mine = z % CLASSES
    two = 2 - 4 * (p % 2)
    two_x = 2 - 4 * (x % 2)
    q = (p + 2) % PLANE
    mate = p + 1 - 2 * (p % 2)

    def at_device(hop, plane, day):
        return lax.rem(z + hop + NZ, NZ) * PLANE + plane, day

    def day_at(k):
        return lax.rem(x + k, NX) * 2 + yh

    def each(low, high, step):
        def body(n, _):
            step(n)
            return 0
        lax.fori_loop(low, high, body, 0)

    def load_rows(n):
        g = lax.rem(x + 1 + n, NX)
        return pltpu.make_async_copy(
            x_hbm.at[0, pl.ds(pl.multiple_of(g * 16, 16), 16)], x_ref.at[g], load.at[n])

    load_table = pltpu.make_async_copy(table_hbm, table, load.at[NX])

    barrier = pltpu.get_barrier_semaphore()

    def greet(device):
        pl.semaphore_signal(barrier, 1, device_id=device, device_id_type=MESH)

    spots = ((two, q), (two, p), (1, q), (-1, q), (1, p), (-1, p), (0, q))
    for j in (1, 3):
        greet(at_device(CLASSES * j, p, d))
    each(0, NX, lambda n: load_rows(n).start())
    load_table.start()

    def greet_sources(plane):
        for hop in (-two, -1, 1):
            greet(at_device(hop, plane, p * 2 + yh))

        @pl.when(jnp.logical_or(plane != p, p != x))
        def _():
            greet(at_device(0, plane, p * 2 + yh))

    each(0, PLANE, greet_sources)
    for hop, plane in spots:
        greet(at_device(-hop, plane, d))
    each(1, NX, lambda k: greet(at_device(0, p, day_at(k))))
    greet(at_device(0, mate, d))
    greet(at_device(0, p, x * 2 + 1 - yh))
    load_table.wait()

    hops = (0, 1, -1, two_x)

    def first_copy(i, k):
        to_class = lax.rem(z + hops[i] + NZ, CLASSES)
        return pltpu.make_async_remote_copy(
            gathered.at[x, lax.rem(x + k, NX), pl.ds(to_class * PER, PER)], first.at[i * PLANE + p],
            first_s.at[i * NX + k], first_r.at[i * PLANE + p],
            device_id=at_device(hops[i], x, day_at(k)), device_id_type=MESH)

    def whiten(n):
        g = lax.rem(x + 1 + n, NX)
        load_rows(n).wait()
        rows = x_ref[g]
        centered = rows - jnp.sum(rows, axis=1, keepdims=True) * (1.0 / SEG)
        rms = jnp.sqrt(jnp.sum(centered * centered, axis=1, keepdims=True) * (1.0 / SEG) + 1e-05)
        live = (16 * g + lax.broadcasted_iota(jnp.int32, (16, 1), 0) < table[b]).astype(F32)
        wide[:, K - 128:] = jnp.zeros((16, 128), F32)
        wide[:, :SEG] = jnp.clip(centered * (1.0 / rms), -CLIP, CLIP) * live
        for i in range(TILES):
            gathered[x, g, i] = wide[:, 128 * i:128 * i + 128].astype(BF16)
        gathered[x, g, TILES] = jnp.zeros((16, 128), BF16)

    each(0, NX, whiten)
    pl.semaphore_wait(barrier, 30 - (p == x).astype(jnp.int32))
    pl.semaphore_signal(token, 1, device_id=at_device(-CLASSES, p, d), device_id_type=MESH)

    def send_first(n):
        k = lax.rem(n + 2, NX)
        for i in (3, 1, 2):
            first_copy(i, k).start()

        @pl.when(jnp.logical_or(k != 0, p != x))
        def _():
            first_copy(0, k).start()

    each(0, NX, send_first)

    @pl.when(p == x)
    def _():
        first[p] = gathered[x, x, pl.ds(mine * PER, PER)]

    def own_copy(k):
        return pltpu.make_async_remote_copy(
            gathered.at[x], gathered.at[x], own_s.at[k], own_r.at[x],
            device_id=at_device(0, p, day_at(k)), device_id_type=MESH)

    each(1, NX, lambda k: own_copy(k).start())

    def shifts_of_day(day):
        def group(g, _):
            rows = jnp.concatenate([gathered[day, g, i] for i in range(TILES)], axis=1)
            for r in range(OWN_SHIFTS):
                rolled = rows if r == 0 else pltpu.roll(rows, r, 1)
                at = pl.multiple_of(r * CAP + g * 16, 16)
                shifted[day % 2, pl.ds(at, 16), pl.ds(pl.multiple_of(day // 2 * K, 128), K)] = rolled
            return 0
        lax.fori_loop(0, CAP // 16, group, 0)

    def own_shifts(k):
        day = lax.rem(x + NX - k, NX)
        pltpu.make_async_remote_copy(
            gathered.at[day], gathered.at[day], own_s.at[k], own_r.at[day],
            device_id=(b, d), device_id_type=MESH).wait_recv()
        shifts_of_day(day)

    shifts_of_day(x)

    def wait_first(j):
        @pl.when(jnp.logical_or(p != x, p != j))
        def _():
            pltpu.make_async_remote_copy(
                first.at[j], first.at[j], first_s.at[0], first_r.at[j],
                device_id=(b, d), device_id_type=MESH).wait_recv()

    each(0, CLASSES * PLANE, wait_first)

    def far_copy(s, j):
        return pltpu.make_async_remote_copy(
            far.at[s, z // CLASSES], far.at[s, z // CLASSES], far_s.at[s, j], far_r.at[s, z // CLASSES],
            device_id=at_device(CLASSES * j, p, d), device_id_type=MESH)

    pl.semaphore_wait(token, 1)
    def send_far(s):
        gap = (z - table[N_BLOCK + s] // PLANE + NZ) % NZ
        came = jnp.where(gap == 1, 1, jnp.where(gap == NZ - 1, 2, jnp.where(gap == (two + NZ) % NZ, 3, 0)))
        far[s, z // CLASSES] = first[came * PLANE + table[N_BLOCK + s] % PLANE]
        for j in (2, 1, 3):
            far_copy(s, j).start()

    each(0, STEPS, send_far)

    def piece(s, part, cls, sem, to):
        return pltpu.make_async_remote_copy(
            full.at[s, part, cls], full.at[s, part, cls], sem, full_r.at[s * PLANE + part, cls],
            device_id=to, device_id_type=MESH)

    core = at_device(0, mate, d)

    def spread(s, j):
        hop, plane = spots[j]
        return piece(s, p, mine, line_s.at[s, j], at_device(hop, plane, d))

    def arrival(s, part, cls):
        piece(s, part, cls, line_s.at[0, 0], (b, d)).wait_recv()

    def core_copy(s, part):
        return pltpu.make_async_remote_copy(
            full.at[s, part], full.at[s, part], core_s.at[s, part], core_r.at[s, part],
            device_id=core, device_id_type=MESH)

    others = [lax.rem(z + k, CLASSES) for k in (1, 3, 2)]

    def open_owner(s):
        for j in (1, 3, 2):
            src = lax.rem(z // CLASSES + j, CLASSES)
            pltpu.make_async_remote_copy(
                far.at[s, src], far.at[s, src], far_s.at[s, j], far_r.at[s, src],
                device_id=(b, d), device_id_type=MESH).wait_recv()
        owner_z = table[N_BLOCK + s] // PLANE
        gap = (mine - owner_z + NZ) % CLASSES
        step = jnp.where(gap == 3, -1, jnp.where(gap == 2, two, gap))
        sender = (owner_z + step + NZ) % NZ
        best = far[s, 0]
        for n in range(1, CLASSES):
            best = jnp.where(sender // CLASSES == n, far[s, n], best)
        full[s, p, mine] = best
        for j in range(len(spots)):
            spread(s, j).start()

    def pass_on(s):
        for cls in others:
            arrival(s, p, cls)
        core_copy(s, p).start()
        arrival(s, q, mine)
        for cls in others:
            arrival(s, q, cls)
        core_copy(s, q).start()

    def from_core(s):
        for part in (mate, (mate + 2) % PLANE):
            core_copy(s, part).wait_recv()

    def add_days(s, odd):
        left = []
        for k in range(2):
            rows = jnp.concatenate(
                [full[s, odd + 2 * k, t // PER, t % PER] for t in range(TILES)], axis=1)
            left.append(jnp.concatenate(
                [pltpu.roll(rows, (HALF - OWN_SHIFTS * n) % K, 1) for n in range(OWNER_SHIFTS)], axis=0))
        return lax.dot_general(jnp.concatenate(left, axis=1), shifted[odd], (((1,), (1,)), ((), ())),
                               preferred_element_type=F32)

    def sum_copy(s):
        return pltpu.make_async_remote_copy(
            outgoing.at[s], incoming.at[s], sum_s.at[s], sum_r.at[s],
            device_id=at_device(0, p, x * 2 + 1 - yh), device_id_type=MESH)

    def halves(s):
        whole = acc[s].reshape(OWNER_SHIFTS, 2, SHARE // 2, COLS)
        return whole[:, 0].reshape(ROWS, COLS), whole[:, 1].reshape(ROWS, COLS)

    def to_partner(s):
        top, low = halves(s)
        outgoing[s] = jnp.where(yh == 0, low, top).astype(BF16)
        sum_copy(s).start()

    def finish(s):
        sum_copy(s).wait_recv()
        top, low = halves(s)
        out_ref[s] = (jnp.where(yh == 0, top, low) + incoming[s].astype(F32)) * (float(DAYS * SEG) ** -0.5)

    each(0, STEPS, open_owner)
    each(1, NX, own_shifts)
    pass_on(0)

    def owner(s):
        def part(h):
            @pl.when(h == 1)
            def _():
                @pl.when(s < STEPS - 1)
                def _():
                    pass_on(s + 1)
                from_core(s)
            sums = add_days(s, lax.rem(p + h, 2))

            @pl.when(h == 0)
            def _():
                acc[s] = sums

            @pl.when(h == 1)
            def _():
                acc[s] += sums
        each(0, 2, part)
        to_partner(s)

    each(0, STEPS, owner)

    def sent(k):
        for i in range(1, CLASSES):
            first_copy(i, k).wait_send()

        @pl.when(jnp.logical_or(k != 0, p != x))
        def _():
            first_copy(0, k).wait_send()

        @pl.when(k > 0)
        def _():
            own_copy(k).wait_send()

    def owner_sent(s):
        for k in range(1, NX):
            far_copy(s, k).wait_send()
        for j in range(len(spots)):
            spread(s, j).wait_send()
        for part in (p, q):
            core_copy(s, part).wait_send()

    each(0, NX, sent)
    each(0, STEPS, owner_sent)
    each(0, STEPS, finish)

    def done(s):
        sum_copy(s).wait_send()

    each(0, STEPS, done)


def per_device(traces, counts, order):
    dma = pltpu.SemaphoreType.DMA
    tile = (16, 128)
    raw = pl.pallas_call(
        kernel,
        out_shape=jax.ShapeDtypeStruct((STEPS, ROWS, COLS), F32),
        in_specs=[pl.BlockSpec(memory_space=pltpu.HBM)] * 2,
        out_specs=pl.BlockSpec(memory_space=pltpu.VMEM),
        scratch_shapes=[
            pltpu.SMEM((2 * N_BLOCK,), jnp.int32),
            pltpu.VMEM((NX, 16, SEG), F32),
            pltpu.VMEM((16, K), F32),
            pltpu.VMEM((NX, NX, TILES + 1) + tile, BF16),
            pltpu.VMEM((CLASSES * PLANE, PER) + tile, BF16),
            pltpu.VMEM((STEPS, CLASSES, PER) + tile, BF16),
            pltpu.VMEM((STEPS, PLANE, CLASSES, PER) + tile, BF16),
            pltpu.VMEM((2, COLS, 2 * K), BF16),
            pltpu.VMEM((STEPS, 2 * ROWS, COLS), F32),
            pltpu.VMEM((STEPS, ROWS, COLS), BF16),
            pltpu.VMEM((STEPS, ROWS, COLS), BF16),
            dma((NX + 1,)), dma((CLASSES * NX,)), dma((CLASSES * PLANE,)), dma((NX,)), dma((NX,)),
            dma((STEPS, CLASSES)), dma((STEPS, CLASSES)), dma((STEPS * PLANE, CLASSES)),
            dma((STEPS, 7)), dma((STEPS, PLANE)), dma((STEPS, PLANE)), dma((STEPS,)), dma((STEPS,)),
            pltpu.SemaphoreType.REGULAR,
        ],
        compiler_params=pltpu.CompilerParams(
            collective_id=0, has_side_effects=True, vmem_limit_bytes=54800 << 10),
        cost_estimate=pl.CostEstimate(flops=2 * STEPS * ROWS * COLS * K * DAYS, bytes_accessed=1 << 20, transcendentals=0),
        name="correlate",
    )(jnp.concatenate([counts, order]), traces)
    parts = raw.reshape(STEPS, OWNER_SHIFTS, SHARE // 2, OWN_SHIFTS, CAP)
    lags = parts.transpose(0, 2, 1, 3, 4).reshape(STEPS, SHARE // 2, OWNER_SHIFTS * OWN_SHIFTS, CAP)
    return lags[:, :, :LAGS]


def solution(mesh):
    return jax.shard_map(
        per_device, mesh=mesh, in_specs=(P("day", "block", None), P(), P()),
        out_specs=P(None, "day", None, "block"), check_vma=False)
```
